32 devices in a mesh: outer: 4 (over y, x), inner: 8 (over z, core).
Axes of the slice: x: 2, y: 2, z: 4, core: 2. Of those that a mesh axis runs over, the one named last changes fastest.
Arguments:
- events: bfloat16 [16, 262144], P(None, ('outer', 'inner')), may hold values from -6 to 6
- coeffs: bfloat16 [64, 262144], P(None, ('outer', 'inner')), may hold values from -6 to 6
- tree_perm: int32 [32, 8192], P(('outer', 'inner')), may hold values from 0 to 8191, each once within a row
- near_list: int32 [512, 32], P(('outer', 'inner')), may hold values from 0 to 511, as said below
- near_count: int32 [512], P(('outer', 'inner')), may hold values from 1 to 32, as said below
- far_list: int32 [512, 4], P(('outer', 'inner')), may hold values from 0 to 7, as said below
- skel_low: int32 [32, 128], P(('outer', 'inner')), may hold values from 0 to 8191, as said below
- skel_high: int32 [4, 128], P('outer'), may hold values from 0 to 1023, as said below
Outputs:
- product: bfloat16 [64, 262144], P(None, ('outer', 'inner'))
The draws below stay inside these ranges and needn't reach their ends.
Inputs may be any that keep to these rules, and one draw needn't show every extreme that they name: `near_list`: slot 0 of leaf i is i; the first near_count[i] slots are distinct leaves within 8 leaves of the leaf's own lower node (i // 16) on either side; the other slots repeat i. `near_count`: some leaf has all 32 slots live. `far_list`: distinct within a leaf, never the leaf's own lower node nor the ones next to it. `skel_low`: distinct within a row. `skel_high`: distinct within a row.
All inputs are finite; a program needn't handle non-finite values.
Results may differ from the reference program's by a relative error of at most 0.006.
Values may be sent and summed in bfloat16 or wider, within the bound.
A program may use at most 64 MiB of HBM per device.

```python
import jax
import jax.numpy as jnp
from jax import lax

FEAT = 16
COLS = 64
LEAF = 512
RANK = 128
NEAR = 32
LEAF_DEV = 16
REACH = 8
GROUPS = 4
GROUP_DEVS = 8
NODES = 32
FAR = 4
EV_DEV = 8192
LEAVES = 512
EVENTS = 262144


def near_plan(key):
    leaf = jnp.arange(LEAVES, dtype=jnp.int32)
    node = leaf // LEAF_DEV
    base = jax.random.randint(jax.random.fold_in(key, 101), (LEAVES,), 2, 7)
    heavy = jax.random.randint(jax.random.fold_in(key, 102), (LEAVES,), 0, 16) == 0
    heavy_val = jax.random.randint(jax.random.fold_in(key, 103), (LEAVES,), 3 * NEAR // 4, NEAR + 1)
    count = jnp.where(heavy, heavy_val, base)
    pick_node = jax.random.randint(jax.random.fold_in(key, 104), (), 1, NODES - 1)
    pick_leaf = jax.random.randint(jax.random.fold_in(key, 105), (), 0, LEAF_DEV)
    count = jnp.where(leaf == pick_node * LEAF_DEV + pick_leaf, NEAR, count)
    width = 2 * LEAF_DEV
    offs = jnp.arange(width, dtype=jnp.int32)
    cand = node[:, None] * LEAF_DEV - REACH + offs[None, :]
    valid = (cand >= 0) & (cand < LEAVES)
    scores = jax.random.randint(jax.random.fold_in(key, 106), (LEAVES, width), 0, 2 ** 20) * width + offs[None, :]
    scores = jnp.where(cand == leaf[:, None], 2 ** 30, scores)
    scores = jnp.where(valid, scores, -1 - offs[None, :])
    order = jnp.argsort(-scores, axis=1)[:, :NEAR]
    picked = jnp.take_along_axis(cand, order, axis=1)
    count = jnp.minimum(jnp.minimum(count, jnp.sum(valid, axis=1)), NEAR)
    slots = jnp.arange(NEAR, dtype=jnp.int32)
    lists = jnp.where(slots[None, :] < count[:, None], picked, leaf[:, None])
    return (lists.astype(jnp.int32), count.astype(jnp.int32))


def draw_near_list(key, part):
    return near_plan(key)[0]


def draw_near_count(key, part):
    return near_plan(key)[1]


def draw_far_list(key, part):
    leaf = jnp.arange(LEAVES, dtype=jnp.int32)
    own = leaf // LEAF_DEV % GROUP_DEVS
    cand = jnp.arange(GROUP_DEVS, dtype=jnp.int32)
    allowed = jnp.abs(cand[None, :] - own[:, None]) >= 2
    scores = jax.random.randint(jax.random.fold_in(key, 201), (LEAVES, GROUP_DEVS), 0, 2 ** 20) * GROUP_DEVS + cand[None, :]
    scores = jnp.where(allowed, scores, -1 - cand[None, :])
    order = jnp.argsort(-scores, axis=1)[:, :FAR]
    return order.astype(jnp.int32)


def distinct_rows(key, rows, total, count):
    keys = jax.random.split(key, rows)
    perms = jax.vmap(lambda k: jax.random.permutation(k, total))(keys).astype(jnp.int32)
    top_pos = jnp.argmax(perms[0] == total - 1).astype(jnp.int32)
    low_pos = jnp.argmax(perms[1] == 0).astype(jnp.int32)
    first = jnp.roll(perms[0], -top_pos)
    second = jnp.roll(perms[1], -low_pos)
    perms = perms.at[0].set(first).at[1].set(second)
    return perms[:, :count]


def draw_skel_low(key, part):
    return distinct_rows(jax.random.fold_in(key, 301), NODES, EV_DEV, RANK)


def draw_skel_high(key, part):
    return distinct_rows(jax.random.fold_in(key, 302), GROUPS, GROUP_DEVS * RANK, RANK)


def steps_of(stream_key, dims, pieces, smallest, largest):
    factor_of, own = 1.0, jax.random.fold_in(stream_key, 6)
    for axis_at, blocks in pieces:
        draws = jnp.exp(jax.random.uniform(jax.random.fold_in(own, axis_at), (blocks,), jnp.float32, smallest / len(pieces), largest / len(pieces)))
        factor_of = factor_of * jnp.repeat(draws, dims[axis_at] // blocks).reshape([-1 if axis == axis_at else 1 for axis in range(len(dims))])
    return factor_of


def gaussian(stream_key, shape, scale, bound, cuts=(), held_as=jnp.bfloat16):
    entries = jax.random.normal(stream_key, shape, jnp.float32) * scale
    if len(cuts) > 0:
        entries = steps_of(stream_key, shape, cuts, -0.22, 0.18) * entries
    return jnp.clip(entries, min=-bound, max=bound).astype(held_as)


def setup_inputs(seed: int = 0) -> dict:
    streams_of = jax.random.split(jax.random.key(seed), 9)
    events = gaussian(streams_of[0], (FEAT, EVENTS), 1.0, 6.0, ((1, 32),))
    coeffs = gaussian(streams_of[1], (COLS, EVENTS), 1.0, 6.0, ((1, 32),))
    tree_perm = jax.vmap(lambda own: jax.random.permutation(own, EV_DEV))(jax.random.split(streams_of[2], NODES)).reshape((NODES, EV_DEV)).astype(jnp.int32)
    near_list = draw_near_list(jax.random.fold_in(streams_of[8], 71), 0)
    near_count = draw_near_count(jax.random.fold_in(streams_of[8], 71), 0)
    far_list = draw_far_list(jax.random.fold_in(streams_of[8], 71), 0)
    skel_low = draw_skel_low(jax.random.fold_in(streams_of[8], 71), 0)
    skel_high = draw_skel_high(jax.random.fold_in(streams_of[8], 71), 0)
    return dict(events=events, coeffs=coeffs, tree_perm=tree_perm, near_list=near_list, near_count=near_count, far_list=far_list, skel_low=skel_low, skel_high=skel_high)


def kernel_tile(left, right):
    left = left.astype(jnp.float32)
    right = right.astype(jnp.float32)
    left_sq = jnp.sum(left * left, axis=0)
    right_sq = jnp.sum(right * right, axis=0)
    cross = jnp.dot(left.T, right, precision=lax.Precision.HIGHEST, preferred_element_type=jnp.float32)
    dist = left_sq[:, None] + right_sq[None, :] - 2.0 * cross
    return jnp.exp(dist * (-2.0 / left.shape[0])).astype(jnp.bfloat16)


def near_sum(padded_x, padded_w, x_leaf, row, count, shift):
    leaf_len = x_leaf.shape[1]
    groups = (count + 3) // 4

    def step(turn, total):
        ids = lax.dynamic_slice_in_dim(row, 4 * turn, 4)
        starts = (ids * leaf_len - shift).astype(jnp.int32)
        block_x = jnp.concatenate([lax.dynamic_slice_in_dim(padded_x, starts[j], leaf_len, 1) for j in range(4)], axis=1)
        block_w = jnp.concatenate([lax.dynamic_slice_in_dim(padded_w, starts[j], leaf_len, 1) for j in range(4)], axis=1)
        live = jnp.repeat(4 * turn + jnp.arange(4, dtype=jnp.int32) < count, leaf_len)
        block_w = jnp.where(live[None, :], block_w, jnp.zeros_like(block_w))
        return total + jnp.dot(block_w, kernel_tile(block_x, x_leaf), preferred_element_type=jnp.float32)

    start = jnp.zeros((padded_w.shape[0], leaf_len), jnp.float32)
    return lax.fori_loop(jnp.int32(0), groups.astype(jnp.int32), step, start)


def far_sum(skel_x, skel_w, x_leaf):
    return jnp.dot(skel_w, kernel_tile(skel_x, x_leaf), preferred_element_type=jnp.float32)


def flat_skel(stack):
    return jnp.transpose(stack, (1, 0, 2)).reshape(stack.shape[1], -1)


def reference(events, coeffs, tree_perm, near_list, near_count, far_list, skel_low, skel_high):
    gidx = (jnp.arange(NODES, dtype=jnp.int32)[:, None] * EV_DEV + tree_perm).reshape(-1)
    xt = events[:, gidx]
    wt = coeffs[:, gidx]
    near_scale = 16.0 / (LEAF * NEAR) ** 0.5
    low_scale = 128.0 / (FAR * RANK) ** 0.5
    high_scale = 128.0 / (GROUPS * RANK) ** 0.5

    def lower(node):
        xd = lax.dynamic_slice_in_dim(xt, node * EV_DEV, EV_DEV, 1)
        wd = lax.dynamic_slice_in_dim(wt, node * EV_DEV, EV_DEV, 1)
        xs = xd[:, skel_low[node]]
        term = jnp.dot(wd, kernel_tile(xd, xs), preferred_element_type=jnp.float32) / EV_DEV ** 0.5
        return xs, term.astype(jnp.bfloat16)

    low_x, low_u = lax.map(lower, jnp.arange(NODES, dtype=jnp.int32))
    pools = low_x.reshape(GROUPS, GROUP_DEVS, FEAT, RANK)
    high_x = jnp.stack([flat_skel(pools[o])[:, skel_high[o]] for o in range(GROUPS)])

    def upper(node):
        xd = lax.dynamic_slice_in_dim(xt, node * EV_DEV, EV_DEV, 1)
        wd = lax.dynamic_slice_in_dim(wt, node * EV_DEV, EV_DEV, 1)
        xso = high_x[node // GROUP_DEVS]
        return jnp.dot(wd, kernel_tile(xd, xso), preferred_element_type=jnp.float32) / (EV_DEV * GROUP_DEVS) ** 0.5

    terms = lax.map(upper, jnp.arange(NODES, dtype=jnp.int32))
    high_u = jnp.sum(terms.reshape(GROUPS, GROUP_DEVS, COLS, RANK), axis=1).astype(jnp.bfloat16)
    high_xf = flat_skel(high_x)

    def leaf_out(leaf):
        x_leaf = lax.dynamic_slice_in_dim(xt, leaf * LEAF, LEAF, 1)
        near = near_sum(xt, wt, x_leaf, near_list[leaf], near_count[leaf], jnp.int32(0))
        group = leaf // LEAF_DEV // GROUP_DEVS
        ids = group * GROUP_DEVS + far_list[leaf]
        low = far_sum(flat_skel(low_x[ids]), flat_skel(low_u[ids]), x_leaf)
        keep = jnp.arange(GROUPS, dtype=jnp.int32) != group
        masked = jnp.where(keep[:, None, None], high_u, jnp.zeros_like(high_u))
        high = far_sum(high_xf, flat_skel(masked), x_leaf)
        return (near * near_scale + low * low_scale + high * high_scale).astype(jnp.bfloat16)

    blocks = lax.map(leaf_out, jnp.arange(LEAVES, dtype=jnp.int32))
    return jnp.transpose(blocks, (1, 0, 2)).reshape(COLS, EVENTS)
```

```python
import functools

import jax
import jax.numpy as jnp
import numpy as np
from jax import lax
from jax.experimental import pallas as pl
from jax.experimental.pallas import tpu as pltpu
from jax.sharding import PartitionSpec as P

LEAF = 512
RANK = 128
NEAR = 32
LEAF_DEV = 16
REACH = 8
DEPTH = 64
VMEM_BYTES = 56 * 1024 * 1024
F32 = jnp.float32
BF16 = jnp.bfloat16


def dot(left, right):
    return jnp.dot(left, right, preferred_element_type=F32)


def split3(value):
    high = value.astype(BF16).astype(F32)
    rest = value - high
    mid = rest.astype(BF16).astype(F32)
    low = (rest - mid).astype(BF16).astype(F32)
    return high, mid, low


def norm_rows(x, first):
    scale = np.float32(-2.0 / x.shape[0] * np.log2(np.e))
    high, mid, low = split3(jnp.sum(x * x, axis=0, keepdims=True) * scale)
    row = lax.broadcasted_iota(jnp.int32, (16, x.shape[1]), 0)
    at = 0 if first else 3
    out = jnp.where((row >= 3 - at) & (row < 6 - at), 1.0, 0.0).astype(F32)
    out = jnp.where(row == at, high, out)
    out = jnp.where(row == at + 1, mid, out)
    return jnp.where(row == at + 2, low, out)


def source_columns(x):
    return jnp.concatenate([x, x, x, norm_rows(x, True)], axis=0)


def target_columns(x):
    scale = np.float32(4.0 / x.shape[0] * np.log2(np.e))
    high, mid, low = split3(x * scale)
    return jnp.concatenate([high, mid, low, norm_rows(x, False)], axis=0).astype(BF16)


def add_tile(total, source, target, weights):
    step = 256
    for p in range(0, source.shape[0], step):
        tile = jnp.exp2(dot(source[p : p + step], target)).astype(BF16)
        total = total + dot(weights[:, p : p + step], tile)
    return total


def leaf_at(index):
    return pl.ds(pl.multiple_of(index * LEAF, LEAF), LEAF)


def order_kernel(perm, skel, events, coeffs, xw, src, tgt, own, table, rows, picked):
    ev_dev = events.shape[1]
    feat = events.shape[0]
    cols = coeffs.shape[0]

    @pl.loop(0, ev_dev // LEAF)
    def _(i):
        at = leaf_at(i)
        block = jnp.concatenate(
            [
                events[:, at].astype(F32),
                coeffs[:, at].astype(F32),
                jnp.zeros((128 - feat - cols, LEAF), F32),
            ],
            axis=0,
        )
        table[at, :] = block.T

    @pl.loop(0, ev_dev // 16)
    def _(i):
        for u in range(16):
            j = i * 16 + u
            rows[pl.ds(j, 1), :] = table[pl.ds(perm[j], 1), :]

    @pl.loop(0, RANK // 8)
    def _(i):
        for u in range(8):
            j = i * 8 + u
            picked[pl.ds(j, 1), :] = rows[pl.ds(skel[j], 1), :]

    own_x = picked[...].T[:feat]
    own_target = target_columns(own_x)

    def step(i, total):
        at = leaf_at(i)
        block = rows[at, :].T
        x = block[:feat]
        both = block[: feat + cols].astype(BF16)
        xw[:, at] = both
        tgt[:, at] = target_columns(x)
        source = source_columns(x).T.astype(BF16)
        src[at, :] = source
        return add_tile(total, source, own_target, both[feat:])

    total = lax.fori_loop(0, ev_dev // LEAF, step, jnp.zeros((cols, RANK), F32))
    own[:feat, :] = own_x.astype(BF16)
    own[feat:, :] = (total * np.float32(1.0 / ev_dev**0.5)).astype(BF16)


def upper_kernel(xw, src, low, skel, out):
    nodes, height, _ = low.shape
    feat = 16
    cols = height - feat
    ev_dev = xw.shape[1]
    width = 1024

    group_x = jnp.zeros((feat, RANK), F32)
    for first in range(0, nodes, 8):
        pool = jnp.concatenate([low[first + i, :feat, :] for i in range(8)], axis=1)
        row = lax.broadcasted_iota(jnp.int32, (width, RANK), 0) + first * RANK
        hot = jnp.where(row == skel[...], 1.0, 0.0).astype(BF16)
        group_x = group_x + dot(pool, hot)
    target = target_columns(group_x)

    def step(i, total):
        at = leaf_at(i)
        return add_tile(total, src[at, :], target, xw[feat:, at])

    total = lax.fori_loop(0, ev_dev // LEAF, step, jnp.zeros((cols, RANK), F32))
    out[:feat, :] = group_x.astype(BF16)
    out[feat:, :] = (total * np.float32(1.0 / (ev_dev * nodes) ** 0.5)).astype(BF16)


def near_own_kernel(rel, count, xw, src, tgt, near):
    feat = 16
    cols = xw.shape[0] - feat

    @pl.loop(0, LEAF_DEV)
    def _(leaf):
        at = leaf_at(leaf)
        near[:, at] = jnp.zeros((cols, LEAF), F32)

        @pl.loop(0, count[leaf])
        def _(slot):
            place = rel[leaf, slot]

            @pl.when((place >= 0) & (place < LEAF_DEV))
            def _():
                there = leaf_at(place)
                near[:, at] = add_tile(near[:, at], src[there, :], tgt[:, at], xw[feat:, there])


def near_halo_kernel(rel, count, left, right, tgt, before, near, src, wts):
    feat = 16
    cols = left.shape[0] - feat

    @pl.loop(0, REACH)
    def _(i):
        for side, ref in enumerate((left, right)):
            at = leaf_at(i)
            there = leaf_at(i + side * REACH)
            src[there, :] = source_columns(ref[:feat, at].astype(F32)).T.astype(BF16)
            wts[:, there] = ref[feat:, at]

    @pl.loop(0, LEAF_DEV)
    def _(leaf):
        at = leaf_at(leaf)
        near[:, at] = before[:, at]

        @pl.loop(0, count[leaf])
        def _(slot):
            place = rel[leaf, slot]

            @pl.when((place < 0) | (place >= LEAF_DEV))
            def _():
                there = leaf_at(jnp.where(place < 0, place + REACH, place + REACH - LEAF_DEV))
                near[:, at] = add_tile(near[:, at], src[there, :], tgt[:, at], wts[:, there])


def far_kernel(picks, group, low, high, tgt, near, out, low_src, low_w, high_src, high_w):
    nodes, height, _ = low.shape
    groups = high.shape[0]
    feat = 16
    cols = height - feat
    far = picks.shape[1]

    for i in range(nodes):
        at = slice(i * RANK, (i + 1) * RANK)
        low_src[at, :] = source_columns(low[i, :feat, :].astype(F32)).T.astype(BF16)
        low_w[:, at] = low[i, feat:, :]
    for o in range(groups):
        at = slice(o * RANK, (o + 1) * RANK)
        high_src[at, :] = source_columns(high[o, 0, :feat, :].astype(F32)).T.astype(BF16)

        def add(i, total):
            return total + high[o, i, feat:, :].astype(F32)

        total = lax.fori_loop(0, nodes, add, jnp.zeros((cols, RANK), F32))
        high_w[:, at] = jnp.where(group[0] == o, 0.0, total).astype(BF16)

    near_scale = np.float32(16.0 / (LEAF * NEAR) ** 0.5)
    low_scale = np.float32(128.0 / (far * RANK) ** 0.5)
    high_scale = np.float32(128.0 / (groups * RANK) ** 0.5)

    @pl.loop(0, LEAF_DEV)
    def _(leaf):
        at = leaf_at(leaf)
        target = tgt[:, at]
        total = jnp.zeros((cols, LEAF), F32)
        for first in range(0, far, 2):
            there = [
                pl.ds(pl.multiple_of(picks[leaf, first + f] * RANK, RANK), RANK) for f in range(2)
            ]
            source = jnp.concatenate([low_src[t, :] for t in there], axis=0)
            weights = jnp.concatenate([low_w[:, t] for t in there], axis=1)
            total = add_tile(total, source, target, weights)
        upper = add_tile(jnp.zeros((cols, LEAF), F32), high_src[...], target, high_w[...])
        out[:, at] = (near[:, at] * near_scale + total * low_scale + upper * high_scale).astype(
            BF16
        )


def call(kernel, scalars, vectors, outs, scratch, tiles):
    flops = int(tiles * LEAF * LEAF * 2 * 128)
    specs = [pl.BlockSpec(memory_space=pltpu.SMEM)] * len(scalars)
    specs += [pl.BlockSpec(memory_space=pltpu.VMEM)] * len(vectors)
    return pl.pallas_call(
        kernel,
        out_shape=outs,
        in_specs=specs,
        out_specs=jax.tree.map(lambda _: pl.BlockSpec(memory_space=pltpu.VMEM), outs),
        scratch_shapes=scratch,
        compiler_params=pltpu.CompilerParams(vmem_limit_bytes=VMEM_BYTES),
        cost_estimate=pl.CostEstimate(
            flops=flops, bytes_accessed=8 << 20, transcendentals=int(tiles * LEAF * LEAF)
        ),
    )(*scalars, *vectors)


def per_device(events, coeffs, tree_perm, near_list, near_count, far_list, skel_low, skel_high):
    group_devs = lax.axis_size("inner")
    group_count = lax.axis_size("outer")
    feat, ev_dev = events.shape
    cols = coeffs.shape[0]
    height = feat + cols
    shape = jax.ShapeDtypeStruct
    own_group = lax.axis_index("outer")
    first_leaf = (own_group * group_devs + lax.axis_index("inner")) * LEAF_DEV
    rel = near_list - first_leaf

    xw, src, tgt, own = call(
        order_kernel,
        (tree_perm[0], skel_low[0]),
        (events, coeffs),
        (
            shape((height, ev_dev), BF16),
            shape((ev_dev, DEPTH), BF16),
            shape((DEPTH, ev_dev), BF16),
            shape((height, RANK), BF16),
        ),
        [
            pltpu.VMEM((ev_dev, 128), F32),
            pltpu.VMEM((ev_dev, 128), F32),
            pltpu.VMEM((RANK, 128), F32),
        ],
        4,
    )
    low = lax.all_gather(own, "inner", axis=0, tiled=False)
    axes = ("outer", "inner")
    ends = group_count * group_devs - 1
    reach = REACH * LEAF
    left = lax.ppermute(xw[:, ev_dev - reach :], axes, [(i, i + 1) for i in range(ends)])
    right = lax.ppermute(xw[:, :reach], axes, [(i + 1, i) for i in range(ends)])
    near = call(
        near_own_kernel,
        (rel, near_count),
        (xw, src, tgt),
        shape((cols, ev_dev), F32),
        [],
        50,
    )
    term = call(
        upper_kernel, (), (xw, src, low, skel_high), shape((height, RANK), BF16), [], 4
    )
    high = lax.all_gather(term, axes, axis=0, tiled=False)
    high = high.reshape(group_count, group_devs, height, RANK)
    near = call(
        near_halo_kernel,
        (rel, near_count),
        (left, right, tgt, near),
        shape((cols, ev_dev), F32),
        [pltpu.VMEM((2 * reach, DEPTH), BF16), pltpu.VMEM((cols, 2 * reach), BF16)],
        40,
    )
    return call(
        far_kernel,
        (far_list, own_group.reshape(1).astype(jnp.int32)),
        (low, high, tgt, near),
        shape((cols, ev_dev), BF16),
        [
            pltpu.VMEM((group_devs * RANK, DEPTH), BF16),
            pltpu.VMEM((cols, group_devs * RANK), BF16),
            pltpu.VMEM((group_count * RANK, DEPTH), BF16),
            pltpu.VMEM((cols, group_count * RANK), BF16),
        ],
        32,
    )


def solution(mesh):
    return jax.shard_map(
        per_device,
        mesh=mesh,
        in_specs=(
            P(None, ("outer", "inner")),
            P(None, ("outer", "inner")),
            P(("outer", "inner"), None),
            P(("outer", "inner"), None),
            P(("outer", "inner")),
            P(("outer", "inner"), None),
            P(("outer", "inner"), None),
            P("outer", None),
        ),
        out_specs=P(None, ("outer", "inner")),
        check_vma=False,
    )
```

```python
import functools

import jax
import jax.numpy as jnp
import numpy as np
from jax import lax
from jax.experimental import pallas as pl
from jax.experimental.pallas import tpu as pltpu
from jax.sharding import PartitionSpec as P

LEAF = 512
RANK = 128
NEAR = 32
LEAF_DEV = 16
REACH = 8
DEPTH = 64
VMEM_BYTES = 56 * 1024 * 1024
F32 = jnp.float32
BF16 = jnp.bfloat16


def dot(left, right):
    return jnp.dot(left, right, preferred_element_type=F32)


def split3(value):
    high = value.astype(BF16).astype(F32)
    rest = value - high
    mid = rest.astype(BF16).astype(F32)
    low = (rest - mid).astype(BF16).astype(F32)
    return high, mid, low


def norm_rows(x, first):
    scale = np.float32(-2.0 / x.shape[0] * np.log2(np.e))
    high, mid, low = split3(jnp.sum(x * x, axis=0, keepdims=True) * scale)
    row = lax.broadcasted_iota(jnp.int32, (16, x.shape[1]), 0)
    at = 0 if first else 3
    out = jnp.where((row >= 3 - at) & (row < 6 - at), 1.0, 0.0).astype(F32)
    out = jnp.where(row == at, high, out)
    out = jnp.where(row == at + 1, mid, out)
    return jnp.where(row == at + 2, low, out)


def source_columns(x):
    return jnp.concatenate([x, x, x, norm_rows(x, True)], axis=0)


def target_columns(x):
    scale = np.float32(4.0 / x.shape[0] * np.log2(np.e))
    high, mid, low = split3(x * scale)
    return jnp.concatenate([high, mid, low, norm_rows(x, False)], axis=0).astype(BF16)


def sum_tiles(chunks):
    sums = []
    ahead = dot(chunks[0][0](), chunks[0][1]())
    for i, (_, _, weights) in enumerate(chunks):
        now = ahead
        if i + 1 < len(chunks):
            ahead = dot(chunks[i + 1][0](), chunks[i + 1][1]())
        sums.append(dot(weights(), jnp.exp2(now).astype(BF16)))
    return sums


STEP = 256


def rows_of(ref, start, size=STEP):
    return lambda: ref[pl.ds(pl.multiple_of(start, size), size), :]


def columns_of(ref, start, size=STEP):
    return lambda: ref[:, pl.ds(pl.multiple_of(start, size), size)]


def term_of(src, wts, target, cols):
    block = 2048

    def step(i, total):
        chunks = [
            (
                rows_of(src, i * block + p),
                lambda: target,
                columns_of(wts, i * block + p),
            )
            for p in range(0, block, STEP)
        ]
        return total + sum(sum_tiles(chunks))

    return lax.fori_loop(0, src.shape[0] // block, step, jnp.zeros((cols, RANK), F32))


def leaf_at(index):
    return pl.ds(pl.multiple_of(index * LEAF, LEAF), LEAF)


def order_kernel(perm, skel, events, coeffs, xs, ws, src, tgt, own, table, rows, picked):
    ev_dev = events.shape[1]
    feat = events.shape[0]
    cols = coeffs.shape[0]

    @pl.loop(0, ev_dev // LEAF)
    def _(i):
        at = leaf_at(i)
        block = jnp.concatenate(
            [
                events[:, at].astype(F32),
                coeffs[:, at].astype(F32),
                jnp.zeros((128 - feat - cols, LEAF), F32),
            ],
            axis=0,
        )
        table[at, :] = block.T

    @pl.loop(0, ev_dev // 16)
    def _(i):
        for u in range(16):
            j = i * 16 + u
            rows[pl.ds(j, 1), :] = table[pl.ds(perm[j], 1), :]

    @pl.loop(0, RANK // 8)
    def _(i):
        for u in range(8):
            j = i * 8 + u
            picked[pl.ds(j, 1), :] = rows[pl.ds(skel[j], 1), :]

    own_x = picked[...].T[:feat]
    own_target = target_columns(own_x)

    @pl.loop(0, ev_dev // LEAF)
    def _(i):
        at = leaf_at(i)
        block = rows[at, :].T
        x = block[:feat]
        xs[:, at] = block[:feat].astype(BF16)
        ws[:, at] = block[feat : feat + cols].astype(BF16)
        tgt[:, at] = target_columns(x)
        src[at, :] = source_columns(x).T.astype(BF16)

    total = term_of(src, ws, own_target, cols)
    own[:feat, :] = own_x.astype(BF16)
    own[feat:, :] = (total * np.float32(1.0 / ev_dev**0.5)).astype(BF16)


def exchange_kernel(
    devs,
    picks,
    xs,
    ws,
    src,
    tgt,
    own,
    skel,
    part,
    left_x,
    left_w,
    right_x,
    right_w,
    low,
    terms,
    high,
    low_src,
    low_w,
    high_src,
    high_w,
    halo_send,
    halo_recv,
    low_send,
    low_recv,
    term_send,
    term_recv,
    high_send,
    high_recv,
):
    groups, nodes = devs
    feat, ev_dev = xs.shape
    cols = ws.shape[0]
    far = picks.shape[1]
    leaves = ev_dev // LEAF
    reach = REACH * LEAF
    near_scale = np.float32(16.0 / (LEAF * NEAR) ** 0.5)
    low_scale = np.float32(128.0 / (far * RANK) ** 0.5)
    high_scale = np.float32(128.0 / (groups * RANK) ** 0.5)
    outer = lax.axis_index("outer")
    inner = lax.axis_index("inner")
    me = outer * nodes + inner
    after = lax.rem(me + 1, groups * nodes)
    before = lax.rem(me + groups * nodes - 1, groups * nodes)
    after = (after // nodes, lax.rem(after, nodes))
    before = (before // nodes, lax.rem(before, nodes))
    inners = [(outer, lax.rem(inner + k, nodes)) for k in range(1, nodes)]
    outers = [(lax.rem(outer + k, groups), inner) for k in range(1, groups)]
    mesh_id = pl.DeviceIdType.MESH

    barrier = pltpu.get_barrier_semaphore()
    for device in inners + outers + [after, before]:
        pl.semaphore_signal(barrier, inc=1, device_id=device, device_id_type=mesh_id)
    pl.semaphore_wait(barrier, len(inners) + len(outers) + 2)

    def send(source, target, device, send_sem, recv_sem):
        copy = pltpu.make_async_remote_copy(
            src_ref=source,
            dst_ref=target,
            send_sem=send_sem,
            recv_sem=recv_sem,
            device_id=device,
            device_id_type=mesh_id,
        )
        copy.start()
        return copy

    low_copies = [
        send(own, low.at[k + 1], device, low_send.at[k], low_recv.at[k])
        for k, device in enumerate(inners)
    ]
    low[0] = own[...]
    halo_copies = [
        send(source, target, device, halo_send.at[i], halo_recv.at[i])
        for i, (source, target, device) in enumerate(
            (
                (xs.at[:, pl.ds(ev_dev - reach, reach)], left_x, after),
                (ws.at[:, pl.ds(ev_dev - reach, reach)], left_w, after),
                (xs.at[:, pl.ds(0, reach)], right_x, before),
                (ws.at[:, pl.ds(0, reach)], right_w, before),
            )
        )
    ]

    def own_tiles(first, last):
        @pl.loop(first, last)
        def _(leaf):
            at = leaf_at(leaf)
            chunks = [
                (
                    rows_of(src, leaf * LEAF + p),
                    lambda: tgt[:, at],
                    columns_of(ws, leaf * LEAF + p),
                )
                for p in range(0, LEAF, STEP)
            ]
            part[:, at] = sum(sum_tiles(chunks)) * near_scale

    own_tiles(0, leaves // 2)

    for copy in low_copies:
        copy.wait()
    for k in range(nodes):
        place = lax.rem(inner + nodes - k, nodes)
        low_src[place] = source_columns(low[k, :feat, :].astype(F32)).T.astype(BF16)
        low_w[place] = low[k, feat:, :]
    group_x = jnp.zeros((feat, RANK), F32)
    width = 8 * RANK
    for first in range(0, nodes, 8):
        row = lax.broadcasted_iota(jnp.int32, (width, RANK), 0) + first * RANK
        hot = jnp.where(row == skel[...], 1.0, 0.0).astype(BF16)
        points = low_src[first : first + 8].reshape(width, DEPTH)[:, :feat]
        group_x = group_x + lax.dot_general(
            points, hot, (((0,), (0,)), ((), ())), preferred_element_type=F32
        )
    total = term_of(src, ws, target_columns(group_x), cols)
    terms[0] = (total * np.float32(1.0 / (ev_dev * nodes) ** 0.5)).astype(BF16)
    term_copies = [
        send(terms.at[0], terms.at[k + 1], device, term_send.at[k], term_recv.at[k])
        for k, device in enumerate(inners)
    ]

    @pl.loop(0, leaves)
    def _(leaf):
        at = leaf_at(leaf)
        chunks = []
        for first in range(0, far, 2):
            there = [picks[leaf, first + f] for f in range(2)]
            chunks.append(
                (
                    lambda there=there: jnp.concatenate([low_src[t] for t in there], axis=0),
                    lambda: tgt[:, at],
                    lambda there=there: jnp.concatenate([low_w[t] for t in there], axis=1),
                )
            )
        total = sum(sum_tiles(chunks)) * low_scale
        out_at = part.at[:, at]
        half = leaves // 2

        @pl.when(leaf < half)
        def _():
            out_at[...] = out_at[...] + total

        @pl.when(leaf >= half)
        def _():
            out_at[...] = total

    for copy in term_copies:
        copy.wait()
    total = jnp.zeros((cols, RANK), F32)
    for k in range(nodes):
        total = total + terms[k].astype(F32)
    high[0, :feat, :] = group_x.astype(BF16)
    high[0, feat:, :] = total.astype(BF16)
    high_copies = [
        send(high.at[0], high.at[k + 1], device, high_send.at[k], high_recv.at[k])
        for k, device in enumerate(outers)
    ]

    @pl.loop(leaves // 2, leaves)
    def _(leaf):
        at = leaf_at(leaf)
        chunks = [
            (
                rows_of(src, leaf * LEAF + p),
                lambda: tgt[:, at],
                columns_of(ws, leaf * LEAF + p),
            )
            for p in range(0, LEAF, STEP)
        ]
        part[:, at] = part[:, at] + sum(sum_tiles(chunks)) * near_scale

    for copy in high_copies:
        copy.wait()
    for k in range(1, groups):
        at = slice((k - 1) * RANK, k * RANK)
        high_src[at, :] = source_columns(high[k, :feat, :].astype(F32)).T.astype(BF16)
        high_w[:, at] = high[k, feat:, :]

    @pl.loop(0, leaves)
    def _(leaf):
        at = leaf_at(leaf)
        count = (groups - 1) * RANK
        chunks = [
            (
                lambda p=p: high_src[p : min(p + STEP, count), :],
                lambda: tgt[:, at],
                lambda p=p: high_w[:, p : min(p + STEP, count)],
            )
            for p in range(0, count, STEP)
        ]
        part[:, at] = part[:, at] + sum(sum_tiles(chunks)) * high_scale

    for copy in halo_copies:
        copy.wait()


TURN = 4


def near_kernel(
    rel, count, xs, ws, left_x, left_w, right_x, right_w, src_own, tgt, part, out, src, wts, near,
    places, targets,
):
    leaves = ws.shape[1] // LEAF
    cols = ws.shape[0]
    dummy = leaves + 2 * REACH
    src[REACH * LEAF : (REACH + leaves) * LEAF, :] = src_own[...]
    wts[:, REACH * LEAF : (REACH + leaves) * LEAF] = ws[...]
    wts[:, : REACH * LEAF] = left_w[...]
    wts[:, (REACH + leaves) * LEAF : dummy * LEAF] = right_w[...]
    src[dummy * LEAF :, :] = jnp.zeros((LEAF, DEPTH), BF16)
    wts[:, dummy * LEAF :] = jnp.zeros((cols, LEAF), BF16)

    @pl.loop(0, REACH)
    def _(i):
        for base, ref in ((0, left_x), (REACH + leaves, right_x)):
            x = ref[:, leaf_at(i)].astype(F32)
            src[leaf_at(base + i), :] = source_columns(x).T.astype(BF16)

    near[...] = jnp.zeros(near.shape, F32)

    def list_leaf(leaf, total):
        def list_slot(slot, at):
            places[at] = rel[leaf, slot] + REACH
            targets[at] = leaf
            return at + 1

        return lax.fori_loop(1, count[leaf], list_slot, total)

    pairs = lax.fori_loop(0, leaves, list_leaf, jnp.int32(0))
    for u in range(TURN):
        places[pairs + u] = dummy
        targets[pairs + u] = 0

    @pl.loop(0, lax.div(pairs + TURN - 1, TURN))
    def _(turn):
        chunks, ats = [], []
        for u in range(TURN):
            place = places[turn * TURN + u]
            at = leaf_at(targets[turn * TURN + u])
            ats.append(at)
            for p in range(0, LEAF, STEP):
                chunks.append(
                    (
                        rows_of(src, place * LEAF + p),
                        lambda at=at: tgt[:, at],
                        columns_of(wts, place * LEAF + p),
                    )
                )
        sums = sum_tiles(chunks)
        each = LEAF // STEP
        for u, at in enumerate(ats):
            near[:, at] += sum(sums[u * each : (u + 1) * each])

    near_scale = np.float32(16.0 / (LEAF * NEAR) ** 0.5)

    @pl.loop(0, leaves)
    def _(leaf):
        at = leaf_at(leaf)
        out[:, at] = (near[:, at] * near_scale + part[:, at]).astype(BF16)


def call(kernel, scalars, vectors, outs, scratch, tiles, collective_id=None):
    flops = int(tiles * LEAF * LEAF * 2 * 128)
    specs = [pl.BlockSpec(memory_space=pltpu.SMEM)] * len(scalars)
    specs += [pl.BlockSpec(memory_space=pltpu.VMEM)] * len(vectors)
    return pl.pallas_call(
        kernel,
        out_shape=outs,
        in_specs=specs,
        out_specs=jax.tree.map(lambda _: pl.BlockSpec(memory_space=pltpu.VMEM), outs),
        scratch_shapes=scratch,
        compiler_params=pltpu.CompilerParams(
            vmem_limit_bytes=VMEM_BYTES,
            collective_id=collective_id,
            has_side_effects=collective_id is not None,
        ),
        cost_estimate=pl.CostEstimate(
            flops=flops, bytes_accessed=8 << 20, transcendentals=int(tiles * LEAF * LEAF)
        ),
    )(*scalars, *vectors)


def per_device(events, coeffs, tree_perm, near_list, near_count, far_list, skel_low, skel_high):
    group_devs = lax.axis_size("inner")
    group_count = lax.axis_size("outer")
    feat, ev_dev = events.shape
    cols = coeffs.shape[0]
    height = feat + cols
    shape = jax.ShapeDtypeStruct
    own_group = lax.axis_index("outer")
    first_leaf = (own_group * group_devs + lax.axis_index("inner")) * LEAF_DEV
    rel = near_list - first_leaf

    xs, ws, src, tgt, own = call(
        order_kernel,
        (tree_perm[0], skel_low[0]),
        (events, coeffs),
        (
            shape((feat, ev_dev), BF16),
            shape((cols, ev_dev), BF16),
            shape((ev_dev, DEPTH), BF16),
            shape((DEPTH, ev_dev), BF16),
            shape((height, RANK), BF16),
        ),
        [
            pltpu.VMEM((ev_dev, 128), F32),
            pltpu.VMEM((ev_dev, 128), F32),
            pltpu.VMEM((RANK, 128), F32),
        ],
        4,
    )
    reach = REACH * LEAF
    sems = [4, 4] + [group_devs - 1] * 4 + [group_count - 1] * 2
    part, *halo = call(
        functools.partial(exchange_kernel, (group_count, group_devs)),
        (far_list,),
        (xs, ws, src, tgt, own, skel_high),
        (
            shape((cols, ev_dev), F32),
            shape((feat, reach), BF16),
            shape((cols, reach), BF16),
            shape((feat, reach), BF16),
            shape((cols, reach), BF16),
        ),
        [
            pltpu.VMEM((group_devs, height, RANK), BF16),
            pltpu.VMEM((group_devs, cols, RANK), BF16),
            pltpu.VMEM((group_count, height, RANK), BF16),
            pltpu.VMEM((group_devs, RANK, DEPTH), BF16),
            pltpu.VMEM((group_devs, cols, RANK), BF16),
            pltpu.VMEM(((group_count - 1) * RANK, DEPTH), BF16),
            pltpu.VMEM((cols, (group_count - 1) * RANK), BF16),
        ]
        + [pltpu.SemaphoreType.DMA((n,)) for n in sems],
        52,
        collective_id=0,
    )
    window = ev_dev + 2 * reach + LEAF
    slots = LEAF_DEV * NEAR + TURN
    return call(
        near_kernel,
        (rel, near_count),
        (xs, ws, *halo, src, tgt, part),
        shape((cols, ev_dev), BF16),
        [
            pltpu.VMEM((window, DEPTH), BF16),
            pltpu.VMEM((cols, window), BF16),
            pltpu.VMEM((cols, ev_dev), F32),
            pltpu.SMEM((slots,), jnp.int32),
            pltpu.SMEM((slots,), jnp.int32),
        ],
        100,
    )


def solution(mesh):
    return jax.shard_map(
        per_device,
        mesh=mesh,
        in_specs=(
            P(None, ("outer", "inner")),
            P(None, ("outer", "inner")),
            P(("outer", "inner"), None),
            P(("outer", "inner"), None),
            P(("outer", "inner")),
            P(("outer", "inner"), None),
            P(("outer", "inner"), None),
            P("outer", None),
        ),
        out_specs=P(None, ("outer", "inner")),
        check_vma=False,
    )
```

```python
import functools

import jax
import jax.numpy as jnp
import numpy as np
from jax import lax
from jax.experimental import pallas as pl
from jax.experimental.pallas import tpu as pltpu
from jax.sharding import PartitionSpec as P

LEAF = 512
RANK = 128
NEAR = 32
LEAF_DEV = 16
REACH = 8
DEPTH = 64
VMEM_BYTES = 56 * 1024 * 1024
F32 = jnp.float32
BF16 = jnp.bfloat16


def dot(left, right):
    return jnp.dot(left, right, preferred_element_type=F32)


def split3(value):
    high = value.astype(BF16).astype(F32)
    rest = value - high
    mid = rest.astype(BF16).astype(F32)
    low = (rest - mid).astype(BF16).astype(F32)
    return high, mid, low


def norm_rows(x, first):
    scale = np.float32(-2.0 / x.shape[0] * np.log2(np.e))
    high, mid, low = split3(jnp.sum(x * x, axis=0, keepdims=True) * scale)
    row = lax.broadcasted_iota(jnp.int32, (16, x.shape[1]), 0)
    at = 0 if first else 3
    out = jnp.where((row >= 3 - at) & (row < 6 - at), 1.0, 0.0).astype(F32)
    out = jnp.where(row == at, high, out)
    out = jnp.where(row == at + 1, mid, out)
    return jnp.where(row == at + 2, low, out)


def source_columns(x):
    return jnp.concatenate([x, x, x, norm_rows(x, True)], axis=0)


def target_columns(x):
    scale = np.float32(4.0 / x.shape[0] * np.log2(np.e))
    high, mid, low = split3(x * scale)
    return jnp.concatenate([high, mid, low, norm_rows(x, False)], axis=0).astype(BF16)


def sum_tiles(chunks):
    sums = []
    ahead = dot(chunks[0][0](), chunks[0][1]())
    for i, (_, _, weights) in enumerate(chunks):
        now = ahead
        if i + 1 < len(chunks):
            ahead = dot(chunks[i + 1][0](), chunks[i + 1][1]())
        sums.append(dot(weights(), jnp.exp2(now).astype(BF16)))
    return sums


STEP = 256
TURN = 4


def rows_of(ref, start, size=STEP):
    return lambda: ref[pl.ds(pl.multiple_of(start, size), size), :]


def columns_of(ref, start, size=STEP):
    return lambda: ref[:, pl.ds(pl.multiple_of(start, size), size)]


def term_of(src, wts, target, cols):
    block = 2048

    def step(i, total):
        chunks = [
            (
                rows_of(src, i * block + p),
                lambda: target,
                columns_of(wts, i * block + p),
            )
            for p in range(0, block, STEP)
        ]
        return total + sum(sum_tiles(chunks))

    return lax.fori_loop(0, src.shape[0] // block, step, jnp.zeros((cols, RANK), F32))


def leaf_at(index):
    return pl.ds(pl.multiple_of(index * LEAF, LEAF), LEAF)


def order_kernel(perm, skel, events, coeffs, xs, ws, src, tgt, own, table, rows, picked):
    feat, ev_dev = events.shape
    cols = coeffs.shape[0]
    blocks = ev_dev // LEAF

    @pl.loop(0, blocks)
    def _(i):
        at = leaf_at(i)
        source = source_columns(events[:, at].astype(F32))
        table[at, :] = jnp.concatenate([source, coeffs[:, at].astype(F32)], axis=0).T

    @pl.loop(0, RANK // 8)
    def _(i):
        for u in range(8):
            j = i * 8 + u
            picked[pl.ds(j, 1), :] = table[pl.ds(perm[skel[j]], 1), :]

    own_x = picked[...].T[:feat]
    own_target = target_columns(own_x)

    def gather(i):
        for u in range(LEAF):
            j = i * LEAF + u
            rows[pl.ds(j, 1), :] = table[pl.ds(perm[j], 1), :]

    def finish(i, total):
        at = leaf_at(i)
        block = rows[at, :]
        src[at, :] = block[:, :DEPTH].astype(BF16)
        block = block.T
        xs[:, at] = block[:feat].astype(BF16)
        ws[:, at] = block[DEPTH:].astype(BF16)
        tgt[:, at] = target_columns(block[:feat])
        source = table[at, :][:, :DEPTH].astype(BF16)
        return total + dot(coeffs[:, at], jnp.exp2(dot(source, own_target)).astype(BF16))

    def step(i, total):
        total = finish(i - 1, total)
        gather(i)
        return total

    gather(0)
    total = lax.fori_loop(1, blocks, step, jnp.zeros((cols, RANK), F32))
    total = finish(blocks - 1, total)
    own[:feat, :] = own_x.astype(BF16)
    own[feat:, :] = (total * np.float32(1.0 / ev_dev**0.5)).astype(BF16)


def exchange_kernel(
    devs,
    picks,
    xs,
    ws,
    src,
    tgt,
    own,
    skel,
    part,
    left_x,
    left_w,
    right_x,
    right_w,
    low,
    terms,
    high,
    low_src,
    low_w,
    high_src,
    high_w,
    halo_send,
    halo_recv,
    low_send,
    low_recv,
    term_send,
    term_recv,
    high_send,
    high_recv,
):
    groups, nodes = devs
    feat, ev_dev = xs.shape
    cols = ws.shape[0]
    far = picks.shape[0]
    leaves = ev_dev // LEAF
    reach = REACH * LEAF
    near_scale = 16.0 / (LEAF * NEAR) ** 0.5
    low_scale = np.float32(128.0 / (far * RANK) ** 0.5 / near_scale)
    high_scale = np.float32(128.0 / (groups * RANK) ** 0.5 / near_scale)
    outer = lax.axis_index("outer")
    inner = lax.axis_index("inner")
    me = outer * nodes + inner
    after = lax.rem(me + 1, groups * nodes)
    before = lax.rem(me + groups * nodes - 1, groups * nodes)
    after = (after // nodes, lax.rem(after, nodes))
    before = (before // nodes, lax.rem(before, nodes))
    inners = [(outer, lax.rem(inner + k, nodes)) for k in range(1, nodes)]
    outers = [(lax.rem(outer + k, groups), inner) for k in range(1, groups)]
    mesh_id = pl.DeviceIdType.MESH

    barrier = pltpu.get_barrier_semaphore()
    for device in inners + outers + [after, before]:
        pl.semaphore_signal(barrier, inc=1, device_id=device, device_id_type=mesh_id)
    pl.semaphore_wait(barrier, len(inners) + len(outers) + 2)

    def send(source, target, device, send_sem, recv_sem):
        copy = pltpu.make_async_remote_copy(
            src_ref=source,
            dst_ref=target,
            send_sem=send_sem,
            recv_sem=recv_sem,
            device_id=device,
            device_id_type=mesh_id,
        )
        copy.start()
        return copy

    low_copies = [
        send(own, low.at[k + 1], device, low_send.at[k], low_recv.at[k])
        for k, device in enumerate(inners)
    ]
    low[0] = own[...]
    halo_copies = [
        send(source, target, device, halo_send.at[i], halo_recv.at[i])
        for i, (source, target, device) in enumerate(
            (
                (xs.at[:, pl.ds(ev_dev - reach, reach)], left_x, after),
                (ws.at[:, pl.ds(ev_dev - reach, reach)], left_w, after),
                (xs.at[:, pl.ds(0, reach)], right_x, before),
                (ws.at[:, pl.ds(0, reach)], right_w, before),
            )
        )
    ]

    def add_leaves(first, last, chunks_of, scale, fresh):
        @pl.loop(first // TURN, last // TURN)
        def _(turn):
            at = [leaf_at(turn * TURN + u) for u in range(TURN)]
            chunks = [chunks_of(turn * TURN + u, at[u]) for u in range(TURN)]
            sums = sum_tiles([chunk for leaf in chunks for chunk in leaf])
            each = len(chunks[0])
            for u in range(TURN):
                total = sum(sums[u * each : (u + 1) * each])
                total = total if scale is None else total * scale
                part[:, at[u]] = total if fresh else part[:, at[u]] + total

    def own_chunks(leaf, at):
        return [
            (rows_of(src, leaf * LEAF + p), lambda: tgt[:, at], columns_of(ws, leaf * LEAF + p))
            for p in range(0, LEAF, STEP)
        ]

    def low_chunks(leaf, at):
        chunks = []
        for first in range(0, far, 2):
            there = [picks[first + f, leaf] for f in range(2)]
            chunks.append(
                (
                    lambda there=there: jnp.concatenate([low_src[t] for t in there], axis=0),
                    lambda: tgt[:, at],
                    lambda there=there: jnp.concatenate([low_w[t] for t in there], axis=1),
                )
            )
        return chunks

    def high_chunks(leaf, at):
        count = (groups - 1) * RANK
        return [
            (
                lambda p=p: high_src[p : min(p + STEP, count), :],
                lambda: tgt[:, at],
                lambda p=p: high_w[:, p : min(p + STEP, count)],
            )
            for p in range(0, count, STEP)
        ]

    half = leaves // 2
    add_leaves(0, half, own_chunks, None, True)

    for copy in low_copies:
        copy.wait()
    for k in range(nodes):
        place = lax.rem(inner + nodes - k, nodes)
        low_src[place] = source_columns(low[k, :feat, :].astype(F32)).T.astype(BF16)
        low_w[place] = low[k, feat:, :]
    group_x = jnp.zeros((feat, RANK), F32)
    width = 8 * RANK
    for first in range(0, nodes, 8):
        row = lax.broadcasted_iota(jnp.int32, (width, RANK), 0) + first * RANK
        hot = jnp.where(row == skel[...], 1.0, 0.0).astype(BF16)
        points = low_src[first : first + 8].reshape(width, DEPTH)[:, :feat]
        group_x = group_x + lax.dot_general(
            points, hot, (((0,), (0,)), ((), ())), preferred_element_type=F32
        )
    total = term_of(src, ws, target_columns(group_x), cols)
    terms[0] = (total * np.float32(1.0 / (ev_dev * nodes) ** 0.5)).astype(BF16)
    term_copies = [
        send(terms.at[0], terms.at[k + 1], device, term_send.at[k], term_recv.at[k])
        for k, device in enumerate(inners)
    ]

    add_leaves(0, half, low_chunks, low_scale, False)
    add_leaves(half, leaves, low_chunks, low_scale, True)

    for copy in term_copies:
        copy.wait()
    total = jnp.zeros((cols, RANK), F32)
    for k in range(nodes):
        total = total + terms[k].astype(F32)
    high[0, :feat, :] = group_x.astype(BF16)
    high[0, feat:, :] = total.astype(BF16)
    high_copies = [
        send(high.at[0], high.at[k + 1], device, high_send.at[k], high_recv.at[k])
        for k, device in enumerate(outers)
    ]

    add_leaves(half, leaves, own_chunks, None, False)

    for copy in high_copies:
        copy.wait()
    for k in range(1, groups):
        at = slice((k - 1) * RANK, k * RANK)
        high_src[at, :] = source_columns(high[k, :feat, :].astype(F32)).T.astype(BF16)
        high_w[:, at] = high[k, feat:, :]

    add_leaves(0, leaves, high_chunks, high_scale, False)

    for copy in halo_copies:
        copy.wait()


def near_kernel(
    nodes, near_list, count, left_x, right_x, tgt, ws, left_w, right_w, src_own, part, out, src,
    wts, near, places, targets, sems,
):
    leaves = ws.shape[1] // LEAF
    cols = ws.shape[0]
    dummy = leaves + 2 * REACH
    own_at = pl.ds(REACH * LEAF, leaves * LEAF)
    copies = [
        pltpu.make_async_copy(source, target, sems.at[i])
        for i, (source, target) in enumerate(
            (
                (src_own, src.at[own_at, :]),
                (ws, wts.at[:, own_at]),
                (left_w, wts.at[:, pl.ds(0, REACH * LEAF)]),
                (right_w, wts.at[:, pl.ds((REACH + leaves) * LEAF, REACH * LEAF)]),
                (part, near),
            )
        )
    ]
    for copy in copies:
        copy.start()
    src[dummy * LEAF :, :] = jnp.zeros((LEAF, DEPTH), BF16)
    wts[:, dummy * LEAF :] = jnp.zeros((cols, LEAF), BF16)

    @pl.loop(0, REACH)
    def _(i):
        for base, ref in ((0, left_x), (REACH + leaves, right_x)):
            x = ref[:, leaf_at(i)].astype(F32)
            src[leaf_at(base + i), :] = source_columns(x).T.astype(BF16)

    first = (lax.axis_index("outer") * nodes + lax.axis_index("inner")) * leaves - REACH

    def list_leaf(leaf, total):
        def list_slot(slot, at):
            places[at] = near_list[leaf, slot] - first
            targets[at] = leaf
            return at + 1

        return lax.fori_loop(1, count[leaf], list_slot, total)

    pairs = lax.fori_loop(0, leaves, list_leaf, jnp.int32(0))
    for u in range(TURN):
        places[pairs + u] = dummy
        targets[pairs + u] = 0
    for copy in copies:
        copy.wait()

    @pl.loop(0, lax.div(pairs + TURN - 1, TURN))
    def _(turn):
        chunks, ats = [], []
        for u in range(TURN):
            place = places[turn * TURN + u]
            at = leaf_at(targets[turn * TURN + u])
            ats.append(at)
            for p in range(0, LEAF, STEP):
                chunks.append(
                    (
                        rows_of(src, place * LEAF + p),
                        lambda at=at: tgt[:, at],
                        columns_of(wts, place * LEAF + p),
                    )
                )
        sums = sum_tiles(chunks)
        each = LEAF // STEP
        for u, at in enumerate(ats):
            near[:, at] += sum(sums[u * each : (u + 1) * each])

    near_scale = np.float32(16.0 / (LEAF * NEAR) ** 0.5)

    @pl.loop(0, leaves)
    def _(leaf):
        at = leaf_at(leaf)
        out[:, at] = (near[:, at] * near_scale).astype(BF16)


def call(kernel, scalars, vectors, outs, scratch, tiles, collective_id=None, anywhere=()):
    flops = int(tiles * LEAF * LEAF * 2 * 128)
    specs = [pl.BlockSpec(memory_space=pltpu.SMEM)] * len(scalars)
    specs += [pl.BlockSpec(memory_space=pltpu.VMEM)] * len(vectors)
    specs += [pl.BlockSpec(memory_space=pl.ANY)] * len(anywhere)
    return pl.pallas_call(
        kernel,
        out_shape=outs,
        in_specs=specs,
        out_specs=jax.tree.map(lambda _: pl.BlockSpec(memory_space=pltpu.VMEM), outs),
        scratch_shapes=scratch,
        compiler_params=pltpu.CompilerParams(
            vmem_limit_bytes=VMEM_BYTES,
            collective_id=collective_id,
            has_side_effects=collective_id is not None,
        ),
        cost_estimate=pl.CostEstimate(
            flops=flops, bytes_accessed=8 << 20, transcendentals=int(tiles * LEAF * LEAF)
        ),
    )(*scalars, *vectors, *anywhere)


def per_device(events, coeffs, tree_perm, near_list, near_count, far_list, skel_low, skel_high):
    group_devs = lax.axis_size("inner")
    group_count = lax.axis_size("outer")
    feat, ev_dev = events.shape
    cols = coeffs.shape[0]
    height = feat + cols
    shape = jax.ShapeDtypeStruct

    xs, ws, src, tgt, own = call(
        order_kernel,
        (tree_perm[0], skel_low[0]),
        (events, coeffs),
        (
            shape((feat, ev_dev), BF16),
            shape((cols, ev_dev), BF16),
            shape((ev_dev, DEPTH), BF16),
            shape((DEPTH, ev_dev), BF16),
            shape((height, RANK), BF16),
        ),
        [
            pltpu.VMEM((ev_dev, 128), F32),
            pltpu.VMEM((ev_dev, 128), F32),
            pltpu.VMEM((RANK, 128), F32),
        ],
        4,
    )
    reach = REACH * LEAF
    sems = [4, 4] + [group_devs - 1] * 4 + [group_count - 1] * 2
    part, left_x, left_w, right_x, right_w = call(
        functools.partial(exchange_kernel, (group_count, group_devs)),
        (far_list.T,),
        (xs, ws, src, tgt, own, skel_high),
        (
            shape((cols, ev_dev), F32),
            shape((feat, reach), BF16),
            shape((cols, reach), BF16),
            shape((feat, reach), BF16),
            shape((cols, reach), BF16),
        ),
        [
            pltpu.VMEM((group_devs, height, RANK), BF16),
            pltpu.VMEM((group_devs, cols, RANK), BF16),
            pltpu.VMEM((group_count, height, RANK), BF16),
            pltpu.VMEM((group_devs, RANK, DEPTH), BF16),
            pltpu.VMEM((group_devs, cols, RANK), BF16),
            pltpu.VMEM(((group_count - 1) * RANK, DEPTH), BF16),
            pltpu.VMEM((cols, (group_count - 1) * RANK), BF16),
        ]
        + [pltpu.SemaphoreType.DMA((n,)) for n in sems],
        52,
        collective_id=0,
    )
    window = ev_dev + 2 * reach + LEAF
    slots = LEAF_DEV * NEAR + TURN
    return call(
        functools.partial(near_kernel, group_devs),
        (near_list, near_count),
        (left_x, right_x, tgt),
        shape((cols, ev_dev), BF16),
        [
            pltpu.VMEM((window, DEPTH), BF16),
            pltpu.VMEM((cols, window), BF16),
            pltpu.VMEM((cols, ev_dev), F32),
            pltpu.SMEM((slots,), jnp.int32),
            pltpu.SMEM((slots,), jnp.int32),
            pltpu.SemaphoreType.DMA((5,)),
        ],
        100,
        anywhere=(ws, left_w, right_w, src, part),
    )


def solution(mesh):
    return jax.shard_map(
        per_device,
        mesh=mesh,
        in_specs=(
            P(None, ("outer", "inner")),
            P(None, ("outer", "inner")),
            P(("outer", "inner"), None),
            P(("outer", "inner"), None),
            P(("outer", "inner")),
            P(("outer", "inner"), None),
            P(("outer", "inner"), None),
            P("outer", None),
        ),
        out_specs=P(None, ("outer", "inner")),
        check_vma=False,
    )
```

```python
import functools

import jax
import jax.numpy as jnp
import numpy as np
from jax import lax
from jax.experimental import pallas as pl
from jax.experimental.pallas import tpu as pltpu
from jax.sharding import PartitionSpec as P

LEAF = 512
RANK = 128
NEAR = 32
LEAF_DEV = 16
REACH = 8
DEPTH = 64
VMEM_BYTES = 56 * 1024 * 1024
F32 = jnp.float32
BF16 = jnp.bfloat16


def dot(left, right):
    return jnp.dot(left, right, preferred_element_type=F32)


def split3(value):
    high = value.astype(BF16).astype(F32)
    rest = value - high
    mid = rest.astype(BF16).astype(F32)
    low = (rest - mid).astype(BF16).astype(F32)
    return high, mid, low


def norm_rows(x, first):
    scale = np.float32(-2.0 / x.shape[0] * np.log2(np.e))
    high, mid, low = split3(jnp.sum(x * x, axis=0, keepdims=True) * scale)
    row = lax.broadcasted_iota(jnp.int32, (16, x.shape[1]), 0)
    at = 0 if first else 3
    out = jnp.where((row >= 3 - at) & (row < 6 - at), 1.0, 0.0).astype(F32)
    out = jnp.where(row == at, high, out)
    out = jnp.where(row == at + 1, mid, out)
    return jnp.where(row == at + 2, low, out)


def source_columns(x):
    return jnp.concatenate([x, x, x, norm_rows(x, True)], axis=0)


def target_columns(x):
    scale = np.float32(4.0 / x.shape[0] * np.log2(np.e))
    high, mid, low = split3(x * scale)
    return jnp.concatenate([high, mid, low, norm_rows(x, False)], axis=0).astype(BF16)


def sum_tiles(chunks):
    sums = []
    ahead = dot(chunks[0][0](), chunks[0][1]())
    for i, (_, _, weights) in enumerate(chunks):
        now = ahead
        if i + 1 < len(chunks):
            ahead = dot(chunks[i + 1][0](), chunks[i + 1][1]())
        sums.append(dot(weights(), jnp.exp2(now).astype(BF16)))
    return sums


STEP = 256
TURN = 4
PAIRS = 8


def rows_of(ref, start, size=STEP):
    return lambda: ref[pl.ds(pl.multiple_of(start, size), size), :]


def columns_of(ref, start, size=STEP):
    return lambda: ref[:, pl.ds(pl.multiple_of(start, size), size)]


def term_of(src, wts, target, cols):
    block = 2048

    def step(i, total):
        chunks = [
            (
                rows_of(src, i * block + p),
                lambda: target,
                columns_of(wts, i * block + p),
            )
            for p in range(0, block, STEP)
        ]
        return total + sum(sum_tiles(chunks))

    return lax.fori_loop(0, src.shape[0] // block, step, jnp.zeros((cols, RANK), F32))


def leaf_at(index):
    return pl.ds(pl.multiple_of(index * LEAF, LEAF), LEAF)


def order_kernel(perm, skel, events, coeffs, xs, ws, src, tgt, own, table, rows, picked):
    feat, ev_dev = events.shape
    cols = coeffs.shape[0]
    blocks = ev_dev // LEAF

    @pl.loop(0, blocks)
    def _(i):
        at = leaf_at(i)
        source = source_columns(events[:, at].astype(F32))
        table[at, :] = jnp.concatenate([source, coeffs[:, at].astype(F32)], axis=0).T

    @pl.loop(0, RANK // 8)
    def _(i):
        for u in range(8):
            j = i * 8 + u
            picked[pl.ds(j, 1), :] = table[pl.ds(perm[skel[j]], 1), :]

    own_x = picked[...].T[:feat]
    own_target = target_columns(own_x)

    def gather(i):
        for u in range(LEAF):
            j = i * LEAF + u
            rows[pl.ds(j, 1), :] = table[pl.ds(perm[j], 1), :]

    def finish(i, total):
        at = leaf_at(i)
        block = rows[at, :]
        src[at, :] = block[:, :DEPTH].astype(BF16)
        block = block.T
        xs[:, at] = block[:feat].astype(BF16)
        ws[:, at] = block[DEPTH:].astype(BF16)
        tgt[:, at] = target_columns(block[:feat])
        source = table[at, :][:, :DEPTH].astype(BF16)
        return total + dot(coeffs[:, at], jnp.exp2(dot(source, own_target)).astype(BF16))

    def step(i, total):
        total = finish(i - 1, total)
        gather(i)
        return total

    gather(0)
    total = lax.fori_loop(1, blocks, step, jnp.zeros((cols, RANK), F32))
    total = finish(blocks - 1, total)
    own[:feat, :] = own_x.astype(BF16)
    own[feat:, :] = (total * np.float32(1.0 / ev_dev**0.5)).astype(BF16)


def exchange_kernel(
    devs,
    picks,
    xs,
    ws,
    src,
    tgt,
    own,
    skel,
    part,
    halo_src,
    left_w,
    right_w,
    left_x,
    right_x,
    low,
    terms,
    high,
    low_src,
    low_w,
    high_src,
    high_w,
    halo_send,
    halo_recv,
    low_send,
    low_recv,
    term_send,
    term_recv,
    high_send,
    high_recv,
):
    groups, nodes = devs
    feat, ev_dev = xs.shape
    cols = ws.shape[0]
    far = picks.shape[0]
    leaves = ev_dev // LEAF
    reach = REACH * LEAF
    near_scale = 16.0 / (LEAF * NEAR) ** 0.5
    low_scale = np.float32(128.0 / (far * RANK) ** 0.5 / near_scale)
    high_scale = np.float32(128.0 / (groups * RANK) ** 0.5 / near_scale)
    outer = lax.axis_index("outer")
    inner = lax.axis_index("inner")
    me = outer * nodes + inner
    after = lax.rem(me + 1, groups * nodes)
    before = lax.rem(me + groups * nodes - 1, groups * nodes)
    after = (after // nodes, lax.rem(after, nodes))
    before = (before // nodes, lax.rem(before, nodes))
    inners = [(outer, lax.rem(inner + k, nodes)) for k in range(1, nodes)]
    outers = [(lax.rem(outer + k, groups), inner) for k in range(1, groups)]
    mesh_id = pl.DeviceIdType.MESH

    barrier = pltpu.get_barrier_semaphore()
    for device in inners + outers + [after, before]:
        pl.semaphore_signal(barrier, inc=1, device_id=device, device_id_type=mesh_id)
    pl.semaphore_wait(barrier, len(inners) + len(outers) + 2)

    def send(source, target, device, send_sem, recv_sem):
        copy = pltpu.make_async_remote_copy(
            src_ref=source,
            dst_ref=target,
            send_sem=send_sem,
            recv_sem=recv_sem,
            device_id=device,
            device_id_type=mesh_id,
        )
        copy.start()
        return copy

    tail = pl.ds(ev_dev - reach, reach)
    head = pl.ds(0, reach)
    x_copies = [
        send(xs.at[:, tail], left_x, after, halo_send.at[0], halo_recv.at[0]),
        send(xs.at[:, head], right_x, before, halo_send.at[1], halo_recv.at[1]),
    ]
    low_copies = [
        send(own, low.at[k + 1], device, low_send.at[k], low_recv.at[k])
        for k, device in enumerate(inners)
    ]
    low[0] = own[...]
    w_copies = [
        send(ws.at[:, tail], left_w, after, halo_send.at[2], halo_recv.at[2]),
        send(ws.at[:, head], right_w, before, halo_send.at[3], halo_recv.at[3]),
    ]

    def add_leaves(first, last, chunks_of, scale, fresh):
        @pl.loop(first // TURN, last // TURN)
        def _(turn):
            at = [leaf_at(turn * TURN + u) for u in range(TURN)]
            chunks = [chunks_of(turn * TURN + u, at[u]) for u in range(TURN)]
            sums = sum_tiles([chunk for leaf in chunks for chunk in leaf])
            each = len(chunks[0])
            for u in range(TURN):
                total = sum(sums[u * each : (u + 1) * each])
                total = total if scale is None else total * scale
                part[:, at[u]] = total if fresh else part[:, at[u]] + total

    def own_chunks(leaf, at):
        return [
            (rows_of(src, leaf * LEAF + p), lambda: tgt[:, at], columns_of(ws, leaf * LEAF + p))
            for p in range(0, LEAF, STEP)
        ]

    def low_chunks(leaf, at):
        chunks = []
        for first in range(0, far, 2):
            there = [picks[first + f, leaf] for f in range(2)]
            chunks.append(
                (
                    lambda there=there: jnp.concatenate([low_src[t] for t in there], axis=0),
                    lambda: tgt[:, at],
                    lambda there=there: jnp.concatenate([low_w[t] for t in there], axis=1),
                )
            )
        return chunks

    def high_chunks(leaf, at):
        count = (groups - 1) * RANK
        return [
            (
                lambda p=p: high_src[p : min(p + STEP, count), :],
                lambda: tgt[:, at],
                lambda p=p: high_w[:, p : min(p + STEP, count)],
            )
            for p in range(0, count, STEP)
        ]

    half = leaves // 2
    add_leaves(0, half, own_chunks, None, True)

    for copy in low_copies:
        copy.wait()
    for k in range(nodes):
        place = lax.rem(inner + nodes - k, nodes)
        low_src[place] = source_columns(low[k, :feat, :].astype(F32)).T.astype(BF16)
        low_w[place] = low[k, feat:, :]
    group_x = jnp.zeros((feat, RANK), F32)
    width = 8 * RANK
    for first in range(0, nodes, 8):
        row = lax.broadcasted_iota(jnp.int32, (width, RANK), 0) + first * RANK
        hot = jnp.where(row == skel[...], 1.0, 0.0).astype(BF16)
        points = low_src[first : first + 8].reshape(width, DEPTH)[:, :feat]
        group_x = group_x + lax.dot_general(
            points, hot, (((0,), (0,)), ((), ())), preferred_element_type=F32
        )
    total = term_of(src, ws, target_columns(group_x), cols)
    terms[0] = (total * np.float32(1.0 / (ev_dev * nodes) ** 0.5)).astype(BF16)
    term_copies = [
        send(terms.at[0], terms.at[k + 1], device, term_send.at[k], term_recv.at[k])
        for k, device in enumerate(inners)
    ]

    add_leaves(0, half, low_chunks, low_scale, False)
    add_leaves(half, leaves, low_chunks, low_scale, True)

    for copy in term_copies:
        copy.wait()
    total = jnp.zeros((cols, RANK), F32)
    for k in range(nodes):
        total = total + terms[k].astype(F32)
    high[0, :feat, :] = group_x.astype(BF16)
    high[0, feat:, :] = total.astype(BF16)
    high_copies = [
        send(high.at[0], high.at[k + 1], device, high_send.at[k], high_recv.at[k])
        for k, device in enumerate(outers)
    ]

    add_leaves(half, leaves, own_chunks, None, False)
    for copy in x_copies:
        copy.wait()

    @pl.loop(0, REACH)
    def _(i):
        for side, ref in enumerate((left_x, right_x)):
            x = ref[:, leaf_at(i)].astype(F32)
            halo_src[leaf_at(side * REACH + i), :] = source_columns(x).T.astype(BF16)

    for copy in high_copies:
        copy.wait()
    for k in range(1, groups):
        at = slice((k - 1) * RANK, k * RANK)
        high_src[at, :] = source_columns(high[k, :feat, :].astype(F32)).T.astype(BF16)
        high_w[:, at] = high[k, feat:, :]

    add_leaves(0, leaves, high_chunks, high_scale, False)

    for copy in w_copies:
        copy.wait()


def near_kernel(
    nodes, near_list, count, tgt, ws, left_w, right_w, src_own, halo_src, part, out, src, wts,
    near, places, targets, sems,
):
    leaves = ws.shape[1] // LEAF
    cols = ws.shape[0]
    dummy = leaves + 2 * REACH
    left_at = pl.ds(0, REACH * LEAF)
    own_at = pl.ds(REACH * LEAF, leaves * LEAF)
    right_at = pl.ds((REACH + leaves) * LEAF, REACH * LEAF)
    copies = [
        pltpu.make_async_copy(source, target, sems.at[i])
        for i, (source, target) in enumerate(
            (
                (src_own, src.at[own_at, :]),
                (halo_src.at[left_at, :], src.at[left_at, :]),
                (halo_src.at[pl.ds(REACH * LEAF, REACH * LEAF), :], src.at[right_at, :]),
                (ws, wts.at[:, own_at]),
                (left_w, wts.at[:, left_at]),
                (right_w, wts.at[:, right_at]),
                (part, near),
            )
        )
    ]
    for copy in copies:
        copy.start()
    src[dummy * LEAF :, :] = jnp.zeros((LEAF, DEPTH), BF16)
    wts[:, dummy * LEAF :] = jnp.zeros((cols, LEAF), BF16)

    first = (lax.axis_index("outer") * nodes + lax.axis_index("inner")) * leaves - REACH

    def list_leaf(leaf, total):
        def list_slot(slot, at):
            places[at] = near_list[leaf, slot] - first
            targets[at] = leaf
            return at + 1

        return lax.fori_loop(1, count[leaf], list_slot, total)

    pairs = lax.fori_loop(0, leaves, list_leaf, jnp.int32(0))
    for u in range(PAIRS):
        places[pairs + u] = dummy
        targets[pairs + u] = 0
    for copy in copies:
        copy.wait()

    @pl.loop(0, lax.div(pairs + PAIRS - 1, PAIRS))
    def _(turn):
        chunks, ats = [], []
        for u in range(PAIRS):
            place = places[turn * PAIRS + u]
            at = leaf_at(targets[turn * PAIRS + u])
            ats.append(at)
            for p in range(0, LEAF, STEP):
                chunks.append(
                    (
                        rows_of(src, place * LEAF + p),
                        lambda at=at: tgt[:, at],
                        columns_of(wts, place * LEAF + p),
                    )
                )
        sums = sum_tiles(chunks)
        each = LEAF // STEP
        for u, at in enumerate(ats):
            near[:, at] += sum(sums[u * each : (u + 1) * each])

    near_scale = np.float32(16.0 / (LEAF * NEAR) ** 0.5)

    @pl.loop(0, leaves)
    def _(leaf):
        at = leaf_at(leaf)
        out[:, at] = (near[:, at] * near_scale).astype(BF16)


def call(kernel, scalars, vectors, outs, scratch, tiles, collective_id=None, anywhere=()):
    flops = int(tiles * LEAF * LEAF * 2 * 128)
    specs = [pl.BlockSpec(memory_space=pltpu.SMEM)] * len(scalars)
    specs += [pl.BlockSpec(memory_space=pltpu.VMEM)] * len(vectors)
    specs += [pl.BlockSpec(memory_space=pl.ANY)] * len(anywhere)
    return pl.pallas_call(
        kernel,
        out_shape=outs,
        in_specs=specs,
        out_specs=jax.tree.map(lambda _: pl.BlockSpec(memory_space=pltpu.VMEM), outs),
        scratch_shapes=scratch,
        compiler_params=pltpu.CompilerParams(
            vmem_limit_bytes=VMEM_BYTES,
            collective_id=collective_id,
            has_side_effects=collective_id is not None,
        ),
        cost_estimate=pl.CostEstimate(
            flops=flops, bytes_accessed=8 << 20, transcendentals=int(tiles * LEAF * LEAF)
        ),
    )(*scalars, *vectors, *anywhere)


def per_device(events, coeffs, tree_perm, near_list, near_count, far_list, skel_low, skel_high):
    group_devs = lax.axis_size("inner")
    group_count = lax.axis_size("outer")
    feat, ev_dev = events.shape
    cols = coeffs.shape[0]
    height = feat + cols
    shape = jax.ShapeDtypeStruct

    xs, ws, src, tgt, own = call(
        order_kernel,
        (tree_perm[0], skel_low[0]),
        (events, coeffs),
        (
            shape((feat, ev_dev), BF16),
            shape((cols, ev_dev), BF16),
            shape((ev_dev, DEPTH), BF16),
            shape((DEPTH, ev_dev), BF16),
            shape((height, RANK), BF16),
        ),
        [
            pltpu.VMEM((ev_dev, 128), F32),
            pltpu.VMEM((ev_dev, 128), F32),
            pltpu.VMEM((RANK, 128), F32),
        ],
        4,
    )
    reach = REACH * LEAF
    sems = [4, 4] + [group_devs - 1] * 4 + [group_count - 1] * 2
    part, halo_src, left_w, right_w = call(
        functools.partial(exchange_kernel, (group_count, group_devs)),
        (far_list.T,),
        (xs, ws, src, tgt, own, skel_high),
        (
            shape((cols, ev_dev), F32),
            shape((2 * reach, DEPTH), BF16),
            shape((cols, reach), BF16),
            shape((cols, reach), BF16),
        ),
        [
            pltpu.VMEM((feat, reach), BF16),
            pltpu.VMEM((feat, reach), BF16),
            pltpu.VMEM((group_devs, height, RANK), BF16),
            pltpu.VMEM((group_devs, cols, RANK), BF16),
            pltpu.VMEM((group_count, height, RANK), BF16),
            pltpu.VMEM((group_devs, RANK, DEPTH), BF16),
            pltpu.VMEM((group_devs, cols, RANK), BF16),
            pltpu.VMEM(((group_count - 1) * RANK, DEPTH), BF16),
            pltpu.VMEM((cols, (group_count - 1) * RANK), BF16),
        ]
        + [pltpu.SemaphoreType.DMA((n,)) for n in sems],
        52,
        collective_id=0,
    )
    window = ev_dev + 2 * reach + LEAF
    slots = LEAF_DEV * NEAR + PAIRS
    return call(
        functools.partial(near_kernel, group_devs),
        (near_list, near_count),
        (tgt,),
        shape((cols, ev_dev), BF16),
        [
            pltpu.VMEM((window, DEPTH), BF16),
            pltpu.VMEM((cols, window), BF16),
            pltpu.VMEM((cols, ev_dev), F32),
            pltpu.SMEM((slots,), jnp.int32),
            pltpu.SMEM((slots,), jnp.int32),
            pltpu.SemaphoreType.DMA((7,)),
        ],
        100,
        anywhere=(ws, left_w, right_w, src, halo_src, part),
    )


def solution(mesh):
    return jax.shard_map(
        per_device,
        mesh=mesh,
        in_specs=(
            P(None, ("outer", "inner")),
            P(None, ("outer", "inner")),
            P(("outer", "inner"), None),
            P(("outer", "inner"), None),
            P(("outer", "inner")),
            P(("outer", "inner"), None),
            P(("outer", "inner"), None),
            P("outer", None),
        ),
        out_specs=P(None, ("outer", "inner")),
        check_vma=False,
    )
```

```python
import functools

import jax
import jax.numpy as jnp
import numpy as np
from jax import lax
from jax.experimental import pallas as pl
from jax.experimental.pallas import tpu as pltpu
from jax.sharding import PartitionSpec as P

LEAF = 512
RANK = 128
NEAR = 32
LEAF_DEV = 16
REACH = 8
SPAN = 64
DEPTH = 128
VMEM_BYTES = 56 * 1024 * 1024
F32 = jnp.float32
BF16 = jnp.bfloat16


def dot(left, right):
    return jnp.dot(left, right, preferred_element_type=F32)


def split3(value):
    high = value.astype(BF16).astype(F32)
    rest = value - high
    mid = rest.astype(BF16).astype(F32)
    low = (rest - mid).astype(BF16).astype(F32)
    return high, mid, low


def norm_rows(x, first):
    scale = np.float32(-2.0 / x.shape[0] * np.log2(np.e))
    high, mid, low = split3(jnp.sum(x * x, axis=0, keepdims=True) * scale)
    row = lax.broadcasted_iota(jnp.int32, (16, x.shape[1]), 0)
    at = 0 if first else 3
    out = jnp.where((row >= 3 - at) & (row < 6 - at), 1.0, 0.0).astype(F32)
    out = jnp.where(row == at, high, out)
    out = jnp.where(row == at + 1, mid, out)
    return jnp.where(row == at + 2, low, out)


def source_columns(x):
    return jnp.concatenate([x, x, x, norm_rows(x, True)], axis=0)


def target_columns(x):
    scale = np.float32(4.0 / x.shape[0] * np.log2(np.e))
    high, mid, low = split3(x * scale)
    zeros = jnp.zeros((DEPTH - SPAN, x.shape[1]), F32)
    return jnp.concatenate([high, mid, low, norm_rows(x, False), zeros], axis=0).astype(BF16)


def source_rows(x):
    zeros = jnp.zeros((DEPTH - SPAN, x.shape[1]), F32)
    return jnp.concatenate([source_columns(x), zeros], axis=0).T.astype(BF16)


def sum_tiles(chunks):
    sums = []
    ahead = dot(chunks[0][0](), chunks[0][1]())
    for i, (_, _, weights) in enumerate(chunks):
        now = ahead
        if i + 1 < len(chunks):
            ahead = dot(chunks[i + 1][0](), chunks[i + 1][1]())
        sums.append(dot(weights(), jnp.exp2(now).astype(BF16)))
    return sums


STEP = 256
TURN = 4
PAIRS = 8


def rows_of(ref, start, size=STEP):
    return lambda: ref[pl.ds(pl.multiple_of(start, size), size), :]


def columns_of(ref, start, size=STEP):
    return lambda: ref[:, pl.ds(pl.multiple_of(start, size), size)]


def term_of(src, wts, target, cols):
    block = 2048

    def step(i, total):
        chunks = [
            (
                rows_of(src, i * block + p),
                lambda: target,
                columns_of(wts, i * block + p),
            )
            for p in range(0, block, STEP)
        ]
        return total + sum(sum_tiles(chunks))

    return lax.fori_loop(0, src.shape[0] // block, step, jnp.zeros((cols, RANK), F32))


def leaf_at(index):
    return pl.ds(pl.multiple_of(index * LEAF, LEAF), LEAF)


def order_kernel(perm, skel, events, coeffs, xs, ws, src, tgt, own, table, rows, picked):
    feat, ev_dev = events.shape
    cols = coeffs.shape[0]
    blocks = ev_dev // LEAF

    @pl.loop(0, blocks)
    def _(i):
        at = leaf_at(i)
        source = source_columns(events[:, at].astype(F32))
        table[at, :] = jnp.concatenate([source, coeffs[:, at].astype(F32)], axis=0).T

    @pl.loop(0, RANK // 8)
    def _(i):
        for u in range(8):
            j = i * 8 + u
            picked[pl.ds(j, 1), :] = table[pl.ds(perm[skel[j]], 1), :]

    own_x = picked[...].T[:feat]
    own_target = target_columns(own_x)

    def gather(i):
        for u in range(LEAF):
            j = i * LEAF + u
            rows[pl.ds(j, 1), :] = table[pl.ds(perm[j], 1), :]

    def finish(i, total):
        at = leaf_at(i)
        block = rows[at, :]
        src[at, :] = block.astype(BF16)
        block = block.T
        xs[:, at] = block[:feat].astype(BF16)
        ws[:, at] = block[SPAN:].astype(BF16)
        tgt[:, at] = target_columns(block[:feat])
        source = table[at, :].astype(BF16)
        return total + dot(coeffs[:, at], jnp.exp2(dot(source, own_target)).astype(BF16))

    def step(i, total):
        total = finish(i - 1, total)
        gather(i)
        return total

    gather(0)
    total = lax.fori_loop(1, blocks, step, jnp.zeros((cols, RANK), F32))
    total = finish(blocks - 1, total)
    own[:feat, :] = own_x.astype(BF16)
    own[feat:, :] = (total * np.float32(1.0 / ev_dev**0.5)).astype(BF16)


def exchange_kernel(
    devs,
    picks,
    xs,
    ws,
    src,
    tgt,
    own,
    skel,
    part,
    halo_src,
    left_w,
    right_w,
    left_x,
    right_x,
    low,
    terms,
    high,
    low_src,
    low_w,
    high_src,
    high_w,
    halo_send,
    halo_recv,
    low_send,
    low_recv,
    term_send,
    term_recv,
    high_send,
    high_recv,
):
    groups, nodes = devs
    feat, ev_dev = xs.shape
    cols = ws.shape[0]
    far = picks.shape[0]
    leaves = ev_dev // LEAF
    reach = REACH * LEAF
    near_scale = 16.0 / (LEAF * NEAR) ** 0.5
    low_scale = np.float32(128.0 / (far * RANK) ** 0.5 / near_scale)
    high_scale = np.float32(128.0 / (groups * RANK) ** 0.5 / near_scale)
    outer = lax.axis_index("outer")
    inner = lax.axis_index("inner")
    me = outer * nodes + inner
    after = lax.rem(me + 1, groups * nodes)
    before = lax.rem(me + groups * nodes - 1, groups * nodes)
    after = (after // nodes, lax.rem(after, nodes))
    before = (before // nodes, lax.rem(before, nodes))
    inners = [(outer, lax.rem(inner + k, nodes)) for k in range(1, nodes)]
    outers = [(lax.rem(outer + k, groups), inner) for k in range(1, groups)]
    mesh_id = pl.DeviceIdType.MESH

    barrier = pltpu.get_barrier_semaphore()
    for device in inners + outers + [after, before]:
        pl.semaphore_signal(barrier, inc=1, device_id=device, device_id_type=mesh_id)
    pl.semaphore_wait(barrier, len(inners) + len(outers) + 2)

    def send(source, target, device, send_sem, recv_sem):
        copy = pltpu.make_async_remote_copy(
            src_ref=source,
            dst_ref=target,
            send_sem=send_sem,
            recv_sem=recv_sem,
            device_id=device,
            device_id_type=mesh_id,
        )
        copy.start()
        return copy

    tail = pl.ds(ev_dev - reach, reach)
    head = pl.ds(0, reach)
    x_copies = [
        send(xs.at[:, tail], left_x, after, halo_send.at[0], halo_recv.at[0]),
        send(xs.at[:, head], right_x, before, halo_send.at[1], halo_recv.at[1]),
    ]
    low_copies = [
        send(own, low.at[k + 1], device, low_send.at[k], low_recv.at[k])
        for k, device in enumerate(inners)
    ]
    low[0] = own[...]
    w_copies = [
        send(ws.at[:, tail], left_w, after, halo_send.at[2], halo_recv.at[2]),
        send(ws.at[:, head], right_w, before, halo_send.at[3], halo_recv.at[3]),
    ]

    def add_leaves(first, last, chunks_of, scale, fresh):
        @pl.loop(first // TURN, last // TURN)
        def _(turn):
            at = [leaf_at(turn * TURN + u) for u in range(TURN)]
            chunks = [chunks_of(turn * TURN + u, at[u]) for u in range(TURN)]
            sums = sum_tiles([chunk for leaf in chunks for chunk in leaf])
            each = len(chunks[0])
            for u in range(TURN):
                total = sum(sums[u * each : (u + 1) * each])
                total = total if scale is None else total * scale
                part[:, at[u]] = total if fresh else part[:, at[u]] + total

    def own_chunks(leaf, at):
        return [
            (rows_of(src, leaf * LEAF + p), lambda: tgt[:, at], columns_of(ws, leaf * LEAF + p))
            for p in range(0, LEAF, STEP)
        ]

    def low_chunks(leaf, at):
        chunks = []
        for first in range(0, far, 2):
            there = [picks[first + f, leaf] for f in range(2)]
            chunks.append(
                (
                    lambda there=there: jnp.concatenate([low_src[t] for t in there], axis=0),
                    lambda: tgt[:, at],
                    lambda there=there: jnp.concatenate([low_w[t] for t in there], axis=1),
                )
            )
        return chunks

    def high_chunks(leaf, at):
        count = (groups - 1) * RANK
        return [
            (
                lambda p=p: high_src[p : min(p + STEP, count), :],
                lambda: tgt[:, at],
                lambda p=p: high_w[:, p : min(p + STEP, count)],
            )
            for p in range(0, count, STEP)
        ]

    half = leaves // 2
    add_leaves(0, half, own_chunks, None, True)

    for copy in low_copies:
        copy.wait()
    for k in range(nodes):
        place = lax.rem(inner + nodes - k, nodes)
        low_src[place] = source_rows(low[k, :feat, :].astype(F32))
        low_w[place] = low[k, feat:, :]
    group_x = jnp.zeros((feat, RANK), F32)
    width = 8 * RANK
    for first in range(0, nodes, 8):
        row = lax.broadcasted_iota(jnp.int32, (width, RANK), 0) + first * RANK
        hot = jnp.where(row == skel[...], 1.0, 0.0).astype(BF16)
        points = low_src[first : first + 8].reshape(width, DEPTH)[:, :feat]
        group_x = group_x + lax.dot_general(
            points, hot, (((0,), (0,)), ((), ())), preferred_element_type=F32
        )
    total = term_of(src, ws, target_columns(group_x), cols)
    terms[0] = (total * np.float32(1.0 / (ev_dev * nodes) ** 0.5)).astype(BF16)
    term_copies = [
        send(terms.at[0], terms.at[k + 1], device, term_send.at[k], term_recv.at[k])
        for k, device in enumerate(inners)
    ]

    add_leaves(0, half, low_chunks, low_scale, False)
    add_leaves(half, leaves, low_chunks, low_scale, True)

    for copy in term_copies:
        copy.wait()
    total = jnp.zeros((cols, RANK), F32)
    for k in range(nodes):
        total = total + terms[k].astype(F32)
    high[0, :feat, :] = group_x.astype(BF16)
    high[0, feat:, :] = total.astype(BF16)
    high_copies = [
        send(high.at[0], high.at[k + 1], device, high_send.at[k], high_recv.at[k])
        for k, device in enumerate(outers)
    ]

    add_leaves(half, leaves, own_chunks, None, False)
    for copy in x_copies:
        copy.wait()

    @pl.loop(0, REACH)
    def _(i):
        for side, ref in enumerate((left_x, right_x)):
            x = ref[:, leaf_at(i)].astype(F32)
            halo_src[leaf_at(side * REACH + i), :] = source_rows(x)

    for copy in high_copies:
        copy.wait()
    for k in range(1, groups):
        at = slice((k - 1) * RANK, k * RANK)
        high_src[at, :] = source_rows(high[k, :feat, :].astype(F32))
        high_w[:, at] = high[k, feat:, :]

    add_leaves(0, leaves, high_chunks, high_scale, False)

    for copy in w_copies:
        copy.wait()


def near_kernel(
    nodes, near_list, count, tgt, ws, left_w, right_w, src_own, halo_src, part, out, src, wts,
    near, places, targets, sems,
):
    leaves = ws.shape[1] // LEAF
    cols = ws.shape[0]
    dummy = leaves + 2 * REACH
    left_at = pl.ds(0, REACH * LEAF)
    own_at = pl.ds(REACH * LEAF, leaves * LEAF)
    right_at = pl.ds((REACH + leaves) * LEAF, REACH * LEAF)
    copies = [
        pltpu.make_async_copy(source, target, sems.at[i])
        for i, (source, target) in enumerate(
            (
                (src_own, src.at[own_at, :]),
                (halo_src.at[left_at, :], src.at[left_at, :]),
                (halo_src.at[pl.ds(REACH * LEAF, REACH * LEAF), :], src.at[right_at, :]),
                (ws, wts.at[:, own_at]),
                (left_w, wts.at[:, left_at]),
                (right_w, wts.at[:, right_at]),
                (part, near),
            )
        )
    ]
    for copy in copies:
        copy.start()
    src[dummy * LEAF :, :] = jnp.zeros((LEAF, DEPTH), BF16)
    wts[:, dummy * LEAF :] = jnp.zeros((cols, LEAF), BF16)

    first = (lax.axis_index("outer") * nodes + lax.axis_index("inner")) * leaves - REACH

    def list_leaf(leaf, total):
        def list_slot(slot, at):
            places[at] = near_list[leaf, slot] - first
            targets[at] = leaf
            return at + 1

        return lax.fori_loop(1, count[leaf], list_slot, total)

    pairs = lax.fori_loop(0, leaves, list_leaf, jnp.int32(0))
    for u in range(PAIRS):
        places[pairs + u] = dummy
        targets[pairs + u] = 0
    for copy in copies:
        copy.wait()

    @pl.loop(0, lax.div(pairs + PAIRS - 1, PAIRS))
    def _(turn):
        chunks, ats = [], []
        for u in range(PAIRS):
            place = places[turn * PAIRS + u]
            at = leaf_at(targets[turn * PAIRS + u])
            ats.append(at)
            for p in range(0, LEAF, STEP):
                chunks.append(
                    (
                        rows_of(src, place * LEAF + p),
                        lambda at=at: tgt[:, at],
                        columns_of(wts, place * LEAF + p),
                    )
                )
        sums = sum_tiles(chunks)
        each = LEAF // STEP
        for u, at in enumerate(ats):
            near[:, at] += sum(sums[u * each : (u + 1) * each])

    near_scale = np.float32(16.0 / (LEAF * NEAR) ** 0.5)

    @pl.loop(0, leaves)
    def _(leaf):
        at = leaf_at(leaf)
        out[:, at] = (near[:, at] * near_scale).astype(BF16)


def call(kernel, scalars, vectors, outs, scratch, tiles, collective_id=None, anywhere=()):
    flops = int(tiles * LEAF * LEAF * 2 * 128)
    specs = [pl.BlockSpec(memory_space=pltpu.SMEM)] * len(scalars)
    specs += [pl.BlockSpec(memory_space=pltpu.VMEM)] * len(vectors)
    specs += [pl.BlockSpec(memory_space=pl.ANY)] * len(anywhere)
    return pl.pallas_call(
        kernel,
        out_shape=outs,
        in_specs=specs,
        out_specs=jax.tree.map(lambda _: pl.BlockSpec(memory_space=pltpu.VMEM), outs),
        scratch_shapes=scratch,
        compiler_params=pltpu.CompilerParams(
            vmem_limit_bytes=VMEM_BYTES,
            collective_id=collective_id,
            has_side_effects=collective_id is not None,
        ),
        cost_estimate=pl.CostEstimate(
            flops=flops, bytes_accessed=8 << 20, transcendentals=int(tiles * LEAF * LEAF)
        ),
    )(*scalars, *vectors, *anywhere)


def per_device(events, coeffs, tree_perm, near_list, near_count, far_list, skel_low, skel_high):
    group_devs = lax.axis_size("inner")
    group_count = lax.axis_size("outer")
    feat, ev_dev = events.shape
    cols = coeffs.shape[0]
    height = feat + cols
    shape = jax.ShapeDtypeStruct

    xs, ws, src, tgt, own = call(
        order_kernel,
        (tree_perm[0], skel_low[0]),
        (events, coeffs),
        (
            shape((feat, ev_dev), BF16),
            shape((cols, ev_dev), BF16),
            shape((ev_dev, DEPTH), BF16),
            shape((DEPTH, ev_dev), BF16),
            shape((height, RANK), BF16),
        ),
        [
            pltpu.VMEM((ev_dev, 128), F32),
            pltpu.VMEM((ev_dev, 128), F32),
            pltpu.VMEM((RANK, 128), F32),
        ],
        4,
    )
    reach = REACH * LEAF
    sems = [4, 4] + [group_devs - 1] * 4 + [group_count - 1] * 2
    part, halo_src, left_w, right_w = call(
        functools.partial(exchange_kernel, (group_count, group_devs)),
        (far_list.T,),
        (xs, ws, src, tgt, own, skel_high),
        (
            shape((cols, ev_dev), F32),
            shape((2 * reach, DEPTH), BF16),
            shape((cols, reach), BF16),
            shape((cols, reach), BF16),
        ),
        [
            pltpu.VMEM((feat, reach), BF16),
            pltpu.VMEM((feat, reach), BF16),
            pltpu.VMEM((group_devs, height, RANK), BF16),
            pltpu.VMEM((group_devs, cols, RANK), BF16),
            pltpu.VMEM((group_count, height, RANK), BF16),
            pltpu.VMEM((group_devs, RANK, DEPTH), BF16),
            pltpu.VMEM((group_devs, cols, RANK), BF16),
            pltpu.VMEM(((group_count - 1) * RANK, DEPTH), BF16),
            pltpu.VMEM((cols, (group_count - 1) * RANK), BF16),
        ]
        + [pltpu.SemaphoreType.DMA((n,)) for n in sems],
        52,
        collective_id=0,
    )
    window = ev_dev + 2 * reach + LEAF
    slots = LEAF_DEV * NEAR + PAIRS
    return call(
        functools.partial(near_kernel, group_devs),
        (near_list, near_count),
        (tgt,),
        shape((cols, ev_dev), BF16),
        [
            pltpu.VMEM((window, DEPTH), BF16),
            pltpu.VMEM((cols, window), BF16),
            pltpu.VMEM((cols, ev_dev), F32),
            pltpu.SMEM((slots,), jnp.int32),
            pltpu.SMEM((slots,), jnp.int32),
            pltpu.SemaphoreType.DMA((7,)),
        ],
        100,
        anywhere=(ws, left_w, right_w, src, halo_src, part),
    )


def solution(mesh):
    return jax.shard_map(
        per_device,
        mesh=mesh,
        in_specs=(
            P(None, ("outer", "inner")),
            P(None, ("outer", "inner")),
            P(("outer", "inner"), None),
            P(("outer", "inner"), None),
            P(("outer", "inner")),
            P(("outer", "inner"), None),
            P(("outer", "inner"), None),
            P("outer", None),
        ),
        out_specs=P(None, ("outer", "inner")),
        check_vma=False,
    )
```

```python
import functools

import jax
import jax.numpy as jnp
import numpy as np
from jax import lax
from jax.experimental import pallas as pl
from jax.experimental.pallas import tpu as pltpu
from jax.sharding import PartitionSpec as P

LEAF = 512
RANK = 128
NEAR = 32
LEAF_DEV = 16
REACH = 8
SPAN = 64
DEPTH = 128
VMEM_BYTES = 56 * 1024 * 1024
F32 = jnp.float32
BF16 = jnp.bfloat16


def dot(left, right):
    return jnp.dot(left, right, preferred_element_type=F32)


def split3(value):
    high = value.astype(BF16).astype(F32)
    rest = value - high
    mid = rest.astype(BF16).astype(F32)
    low = (rest - mid).astype(BF16).astype(F32)
    return high, mid, low


def norm_rows(x, first):
    scale = np.float32(-2.0 / x.shape[0] * np.log2(np.e))
    high, mid, low = split3(jnp.sum(x * x, axis=0, keepdims=True) * scale)
    row = lax.broadcasted_iota(jnp.int32, (16, x.shape[1]), 0)
    at = 0 if first else 3
    out = jnp.where((row >= 3 - at) & (row < 6 - at), 1.0, 0.0).astype(F32)
    out = jnp.where(row == at, high, out)
    out = jnp.where(row == at + 1, mid, out)
    return jnp.where(row == at + 2, low, out)


def source_columns(x):
    return jnp.concatenate([x, x, x, norm_rows(x, True)], axis=0)


def target_columns(x):
    scale = np.float32(4.0 / x.shape[0] * np.log2(np.e))
    high, mid, low = split3(x * scale)
    zeros = jnp.zeros((DEPTH - SPAN, x.shape[1]), F32)
    return jnp.concatenate([high, mid, low, norm_rows(x, False), zeros], axis=0).astype(BF16)


def source_rows(x):
    zeros = jnp.zeros((DEPTH - SPAN, x.shape[1]), F32)
    return jnp.concatenate([source_columns(x), zeros], axis=0).T.astype(BF16)


def sum_tiles(chunks):
    sums = []
    ahead = dot(chunks[0][0](), chunks[0][1]())
    for i, (_, _, weights) in enumerate(chunks):
        now = ahead
        if i + 1 < len(chunks):
            ahead = dot(chunks[i + 1][0](), chunks[i + 1][1]())
        sums.append(dot(weights(), jnp.exp2(now).astype(BF16)))
    return sums


STEP = 256
TURN = 4
PAIRS = 8


def halves_of(leaf):
    return [
        pl.ds(pl.multiple_of(leaf * LEAF + q, STEP), STEP) for q in range(0, LEAF, STEP)
    ]


def rows_of(ref, start, size=STEP):
    return lambda: ref[pl.ds(pl.multiple_of(start, size), size), :]


def columns_of(ref, start, size=STEP):
    return lambda: ref[:, pl.ds(pl.multiple_of(start, size), size)]


def term_of(src, wts, target, cols):
    block = 2048

    def step(i, total):
        chunks = [
            (
                rows_of(src, i * block + p),
                lambda: target,
                columns_of(wts, i * block + p),
            )
            for p in range(0, block, STEP)
        ]
        return total + sum(sum_tiles(chunks))

    return lax.fori_loop(0, src.shape[0] // block, step, jnp.zeros((cols, RANK), F32))


def leaf_at(index):
    return pl.ds(pl.multiple_of(index * LEAF, LEAF), LEAF)


def order_kernel(perm, skel, events, coeffs, xs, ws, src, tgt, own, table, rows, picked):
    feat, ev_dev = events.shape
    cols = coeffs.shape[0]
    blocks = ev_dev // LEAF

    @pl.loop(0, blocks)
    def _(i):
        at = leaf_at(i)
        source = source_columns(events[:, at].astype(F32))
        table[at, :] = jnp.concatenate([source, coeffs[:, at].astype(F32)], axis=0).T

    @pl.loop(0, RANK // 8)
    def _(i):
        for u in range(8):
            j = i * 8 + u
            picked[pl.ds(j, 1), :] = table[pl.ds(perm[skel[j]], 1), :]

    own_x = picked[...].T[:feat]
    own_target = target_columns(own_x)

    def gather(i):
        for u in range(LEAF):
            j = i * LEAF + u
            rows[pl.ds(j, 1), :] = table[pl.ds(perm[j], 1), :]

    def finish(i, total):
        at = leaf_at(i)
        block = rows[at, :]
        src[at, :] = block.astype(BF16)
        block = block.T
        xs[:, at] = block[:feat].astype(BF16)
        ws[:, at] = block[SPAN:].astype(BF16)
        tgt[:, at] = target_columns(block[:feat])
        source = table[at, :].astype(BF16)
        return total + dot(coeffs[:, at], jnp.exp2(dot(source, own_target)).astype(BF16))

    def step(i, total):
        total = finish(i - 1, total)
        gather(i)
        return total

    gather(0)
    total = lax.fori_loop(1, blocks, step, jnp.zeros((cols, RANK), F32))
    total = finish(blocks - 1, total)
    own[:feat, :] = own_x.astype(BF16)
    own[feat:, :] = (total * np.float32(1.0 / ev_dev**0.5)).astype(BF16)


def exchange_kernel(
    devs,
    picks,
    xs,
    ws,
    src,
    tgt,
    own,
    skel,
    part,
    halo_src,
    left_w,
    right_w,
    left_x,
    right_x,
    low,
    terms,
    high,
    low_src,
    low_w,
    high_src,
    high_w,
    halo_send,
    halo_recv,
    low_send,
    low_recv,
    term_send,
    term_recv,
    high_send,
    high_recv,
):
    groups, nodes = devs
    feat, ev_dev = xs.shape
    cols = ws.shape[0]
    far = picks.shape[0]
    leaves = ev_dev // LEAF
    reach = REACH * LEAF
    near_scale = 16.0 / (LEAF * NEAR) ** 0.5
    low_scale = np.float32(128.0 / (far * RANK) ** 0.5 / near_scale)
    high_scale = np.float32(128.0 / (groups * RANK) ** 0.5 / near_scale)
    outer = lax.axis_index("outer")
    inner = lax.axis_index("inner")
    me = outer * nodes + inner
    after = lax.rem(me + 1, groups * nodes)
    before = lax.rem(me + groups * nodes - 1, groups * nodes)
    after = (after // nodes, lax.rem(after, nodes))
    before = (before // nodes, lax.rem(before, nodes))
    inners = [(outer, lax.rem(inner + k, nodes)) for k in range(1, nodes)]
    outers = [(lax.rem(outer + k, groups), inner) for k in range(1, groups)]
    mesh_id = pl.DeviceIdType.MESH

    barrier = pltpu.get_barrier_semaphore()
    for device in inners + outers + [after, before]:
        pl.semaphore_signal(barrier, inc=1, device_id=device, device_id_type=mesh_id)
    pl.semaphore_wait(barrier, len(inners) + len(outers) + 2)

    def send(source, target, device, send_sem, recv_sem):
        copy = pltpu.make_async_remote_copy(
            src_ref=source,
            dst_ref=target,
            send_sem=send_sem,
            recv_sem=recv_sem,
            device_id=device,
            device_id_type=mesh_id,
        )
        copy.start()
        return copy

    tail = pl.ds(ev_dev - reach, reach)
    head = pl.ds(0, reach)
    x_copies = [
        send(xs.at[:, tail], left_x, after, halo_send.at[0], halo_recv.at[0]),
        send(xs.at[:, head], right_x, before, halo_send.at[1], halo_recv.at[1]),
    ]
    low_copies = [
        send(own, low.at[k + 1], device, low_send.at[k], low_recv.at[k])
        for k, device in enumerate(inners)
    ]
    low[0] = own[...]
    w_copies = [
        send(ws.at[:, tail], left_w, after, halo_send.at[2], halo_recv.at[2]),
        send(ws.at[:, head], right_w, before, halo_send.at[3], halo_recv.at[3]),
    ]

    def add_leaves(first, last, chunks_of, scale, fresh):
        @pl.loop(first // TURN, last // TURN)
        def _(turn):
            ats = [
                at for u in range(TURN) for at in halves_of(turn * TURN + u)
            ]
            chunks = [chunks_of(turn * TURN + i * STEP // LEAF, at) for i, at in enumerate(ats)]
            sums = sum_tiles([chunk for one in chunks for chunk in one])
            each = len(chunks[0])
            for i, at in enumerate(ats):
                total = sum(sums[i * each : (i + 1) * each])
                total = total if scale is None else total * scale
                part[:, at] = total if fresh else part[:, at] + total

    def own_chunks(leaf, at):
        return [
            (
                rows_of(src, leaf * LEAF, LEAF),
                lambda: tgt[:, at],
                columns_of(ws, leaf * LEAF, LEAF),
            )
        ]

    def low_chunks(leaf, at):
        chunks = []
        for first in range(0, far, 4):
            there = [picks[first + f, leaf] for f in range(4)]
            chunks.append(
                (
                    lambda there=there: jnp.concatenate([low_src[t] for t in there], axis=0),
                    lambda: tgt[:, at],
                    lambda there=there: jnp.concatenate([low_w[t] for t in there], axis=1),
                )
            )
        return chunks

    def high_chunks(leaf, at):
        return [(lambda: high_src[...], lambda: tgt[:, at], lambda: high_w[...])]

    half = leaves // 2
    add_leaves(0, half, own_chunks, None, True)

    for copy in low_copies:
        copy.wait()
    for k in range(nodes):
        place = lax.rem(inner + nodes - k, nodes)
        low_src[place] = source_rows(low[k, :feat, :].astype(F32))
        low_w[place] = low[k, feat:, :]
    group_x = jnp.zeros((feat, RANK), F32)
    width = 8 * RANK
    for first in range(0, nodes, 8):
        row = lax.broadcasted_iota(jnp.int32, (width, RANK), 0) + first * RANK
        hot = jnp.where(row == skel[...], 1.0, 0.0).astype(BF16)
        points = low_src[first : first + 8].reshape(width, DEPTH)[:, :feat]
        group_x = group_x + lax.dot_general(
            points, hot, (((0,), (0,)), ((), ())), preferred_element_type=F32
        )
    total = term_of(src, ws, target_columns(group_x), cols)
    terms[0] = (total * np.float32(1.0 / (ev_dev * nodes) ** 0.5)).astype(BF16)
    term_copies = [
        send(terms.at[0], terms.at[k + 1], device, term_send.at[k], term_recv.at[k])
        for k, device in enumerate(inners)
    ]

    add_leaves(0, half, low_chunks, low_scale, False)
    add_leaves(half, leaves, low_chunks, low_scale, True)

    for copy in term_copies:
        copy.wait()
    total = jnp.zeros((cols, RANK), F32)
    for k in range(nodes):
        total = total + terms[k].astype(F32)
    high[0, :feat, :] = group_x.astype(BF16)
    high[0, feat:, :] = total.astype(BF16)
    high_copies = [
        send(high.at[0], high.at[k + 1], device, high_send.at[k], high_recv.at[k])
        for k, device in enumerate(outers)
    ]

    add_leaves(half, leaves, own_chunks, None, False)
    for copy in x_copies:
        copy.wait()

    @pl.loop(0, REACH)
    def _(i):
        for side, ref in enumerate((left_x, right_x)):
            x = ref[:, leaf_at(i)].astype(F32)
            halo_src[leaf_at(side * REACH + i), :] = source_rows(x)

    for copy in high_copies:
        copy.wait()
    for k in range(1, groups):
        at = slice((k - 1) * RANK, k * RANK)
        high_src[at, :] = source_rows(high[k, :feat, :].astype(F32))
        high_w[:, at] = high[k, feat:, :]

    add_leaves(0, leaves, high_chunks, high_scale, False)

    for copy in w_copies:
        copy.wait()


def near_kernel(
    nodes, near_list, count, tgt, ws, left_w, right_w, src_own, halo_src, part, out, src, wts,
    near, places, targets, sems,
):
    leaves = ws.shape[1] // LEAF
    cols = ws.shape[0]
    dummy = leaves + 2 * REACH
    left_at = pl.ds(0, REACH * LEAF)
    own_at = pl.ds(REACH * LEAF, leaves * LEAF)
    right_at = pl.ds((REACH + leaves) * LEAF, REACH * LEAF)
    copies = [
        pltpu.make_async_copy(source, target, sems.at[i])
        for i, (source, target) in enumerate(
            (
                (src_own, src.at[own_at, :]),
                (halo_src.at[left_at, :], src.at[left_at, :]),
                (halo_src.at[pl.ds(REACH * LEAF, REACH * LEAF), :], src.at[right_at, :]),
                (ws, wts.at[:, own_at]),
                (left_w, wts.at[:, left_at]),
                (right_w, wts.at[:, right_at]),
                (part, near),
            )
        )
    ]
    for copy in copies:
        copy.start()
    src[dummy * LEAF :, :] = jnp.zeros((LEAF, DEPTH), BF16)
    wts[:, dummy * LEAF :] = jnp.zeros((cols, LEAF), BF16)

    first = (lax.axis_index("outer") * nodes + lax.axis_index("inner")) * leaves - REACH

    def list_leaf(leaf, total):
        def list_slot(slot, at):
            places[at] = near_list[leaf, slot] - first
            targets[at] = leaf
            return at + 1

        return lax.fori_loop(1, count[leaf], list_slot, total)

    pairs = lax.fori_loop(0, leaves, list_leaf, jnp.int32(0))
    for u in range(PAIRS):
        places[pairs + u] = dummy
        targets[pairs + u] = 0
    for copy in copies:
        copy.wait()

    @pl.loop(0, lax.div(pairs + PAIRS - 1, PAIRS))
    def _(turn):
        chunks, ats = [], []
        for u in range(PAIRS):
            place = places[turn * PAIRS + u]
            for at in halves_of(targets[turn * PAIRS + u]):
                ats.append(at)
                chunks.append(
                    (
                        rows_of(src, place * LEAF, LEAF),
                        lambda at=at: tgt[:, at],
                        columns_of(wts, place * LEAF, LEAF),
                    )
                )
        for at, one in zip(ats, sum_tiles(chunks)):
            near[:, at] += one

    near_scale = np.float32(16.0 / (LEAF * NEAR) ** 0.5)

    @pl.loop(0, leaves)
    def _(leaf):
        at = leaf_at(leaf)
        out[:, at] = (near[:, at] * near_scale).astype(BF16)


def call(kernel, scalars, vectors, outs, scratch, tiles, collective_id=None, anywhere=()):
    flops = int(tiles * LEAF * LEAF * 2 * 128)
    specs = [pl.BlockSpec(memory_space=pltpu.SMEM)] * len(scalars)
    specs += [pl.BlockSpec(memory_space=pltpu.VMEM)] * len(vectors)
    specs += [pl.BlockSpec(memory_space=pl.ANY)] * len(anywhere)
    return pl.pallas_call(
        kernel,
        out_shape=outs,
        in_specs=specs,
        out_specs=jax.tree.map(lambda _: pl.BlockSpec(memory_space=pltpu.VMEM), outs),
        scratch_shapes=scratch,
        compiler_params=pltpu.CompilerParams(
            vmem_limit_bytes=VMEM_BYTES,
            collective_id=collective_id,
            has_side_effects=collective_id is not None,
        ),
        cost_estimate=pl.CostEstimate(
            flops=flops, bytes_accessed=8 << 20, transcendentals=int(tiles * LEAF * LEAF)
        ),
    )(*scalars, *vectors, *anywhere)


def per_device(events, coeffs, tree_perm, near_list, near_count, far_list, skel_low, skel_high):
    group_devs = lax.axis_size("inner")
    group_count = lax.axis_size("outer")
    feat, ev_dev = events.shape
    cols = coeffs.shape[0]
    height = feat + cols
    shape = jax.ShapeDtypeStruct

    xs, ws, src, tgt, own = call(
        order_kernel,
        (tree_perm[0], skel_low[0]),
        (events, coeffs),
        (
            shape((feat, ev_dev), BF16),
            shape((cols, ev_dev), BF16),
            shape((ev_dev, DEPTH), BF16),
            shape((DEPTH, ev_dev), BF16),
            shape((height, RANK), BF16),
        ),
        [
            pltpu.VMEM((ev_dev, 128), F32),
            pltpu.VMEM((ev_dev, 128), F32),
            pltpu.VMEM((RANK, 128), F32),
        ],
        4,
    )
    reach = REACH * LEAF
    sems = [4, 4] + [group_devs - 1] * 4 + [group_count - 1] * 2
    part, halo_src, left_w, right_w = call(
        functools.partial(exchange_kernel, (group_count, group_devs)),
        (far_list.T,),
        (xs, ws, src, tgt, own, skel_high),
        (
            shape((cols, ev_dev), F32),
            shape((2 * reach, DEPTH), BF16),
            shape((cols, reach), BF16),
            shape((cols, reach), BF16),
        ),
        [
            pltpu.VMEM((feat, reach), BF16),
            pltpu.VMEM((feat, reach), BF16),
            pltpu.VMEM((group_devs, height, RANK), BF16),
            pltpu.VMEM((group_devs, cols, RANK), BF16),
            pltpu.VMEM((group_count, height, RANK), BF16),
            pltpu.VMEM((group_devs, RANK, DEPTH), BF16),
            pltpu.VMEM((group_devs, cols, RANK), BF16),
            pltpu.VMEM(((group_count - 1) * RANK, DEPTH), BF16),
            pltpu.VMEM((cols, (group_count - 1) * RANK), BF16),
        ]
        + [pltpu.SemaphoreType.DMA((n,)) for n in sems],
        52,
        collective_id=0,
    )
    window = ev_dev + 2 * reach + LEAF
    slots = LEAF_DEV * NEAR + PAIRS
    return call(
        functools.partial(near_kernel, group_devs),
        (near_list, near_count),
        (tgt,),
        shape((cols, ev_dev), BF16),
        [
            pltpu.VMEM((window, DEPTH), BF16),
            pltpu.VMEM((cols, window), BF16),
            pltpu.VMEM((cols, ev_dev), F32),
            pltpu.SMEM((slots,), jnp.int32),
            pltpu.SMEM((slots,), jnp.int32),
            pltpu.SemaphoreType.DMA((7,)),
        ],
        100,
        anywhere=(ws, left_w, right_w, src, halo_src, part),
    )


def solution(mesh):
    return jax.shard_map(
        per_device,
        mesh=mesh,
        in_specs=(
            P(None, ("outer", "inner")),
            P(None, ("outer", "inner")),
            P(("outer", "inner"), None),
            P(("outer", "inner"), None),
            P(("outer", "inner")),
            P(("outer", "inner"), None),
            P(("outer", "inner"), None),
            P("outer", None),
        ),
        out_specs=P(None, ("outer", "inner")),
        check_vma=False,
    )
```

```python
import functools

import jax
import jax.numpy as jnp
import numpy as np
from jax import lax
from jax.experimental import pallas as pl
from jax.experimental.pallas import tpu as pltpu
from jax.sharding import PartitionSpec as P

LEAF = 512
RANK = 128
NEAR = 32
LEAF_DEV = 16
REACH = 8
SPAN = 64
DEPTH = 128
VMEM_BYTES = 56 * 1024 * 1024
F32 = jnp.float32
BF16 = jnp.bfloat16


def dot(left, right):
    return jnp.dot(left, right, preferred_element_type=F32)


def split3(value):
    high = value.astype(BF16).astype(F32)
    rest = value - high
    mid = rest.astype(BF16).astype(F32)
    low = (rest - mid).astype(BF16).astype(F32)
    return high, mid, low


def norm_rows(x, first):
    scale = np.float32(-2.0 / x.shape[0] * np.log2(np.e))
    high, mid, low = split3(jnp.sum(x * x, axis=0, keepdims=True) * scale)
    row = lax.broadcasted_iota(jnp.int32, (16, x.shape[1]), 0)
    at = 0 if first else 3
    out = jnp.where((row >= 3 - at) & (row < 6 - at), 1.0, 0.0).astype(F32)
    out = jnp.where(row == at, high, out)
    out = jnp.where(row == at + 1, mid, out)
    return jnp.where(row == at + 2, low, out)


def source_columns(x):
    return jnp.concatenate([x, x, x, norm_rows(x, True)], axis=0)


def target_columns(x):
    scale = np.float32(4.0 / x.shape[0] * np.log2(np.e))
    high, mid, low = split3(x * scale)
    zeros = jnp.zeros((DEPTH - SPAN, x.shape[1]), F32)
    return jnp.concatenate([high, mid, low, norm_rows(x, False), zeros], axis=0).astype(BF16)


def source_rows(x):
    zeros = jnp.zeros((DEPTH - SPAN, x.shape[1]), F32)
    return jnp.concatenate([source_columns(x), zeros], axis=0).T.astype(BF16)


def sum_tiles(chunks):
    sums = []
    ahead = dot(chunks[0][0](), chunks[0][1]())
    for i, (_, _, weights) in enumerate(chunks):
        now = ahead
        if i + 1 < len(chunks):
            ahead = dot(chunks[i + 1][0](), chunks[i + 1][1]())
        sums.append(dot(weights(), jnp.exp2(now).astype(BF16)))
    return sums


STEP = 256
TURN = 4
PAIRS = 8


def halves_of(leaf):
    return [
        pl.ds(pl.multiple_of(leaf * LEAF + q, STEP), STEP) for q in range(0, LEAF, STEP)
    ]


def rows_of(ref, start, size=STEP):
    return lambda: ref[pl.ds(pl.multiple_of(start, size), size), :]


def columns_of(ref, start, size=STEP):
    return lambda: ref[:, pl.ds(pl.multiple_of(start, size), size)]


def term_of(src, wts, target, cols):
    block = 2048

    def step(i, total):
        chunks = [
            (
                rows_of(src, i * block + p),
                lambda: target,
                columns_of(wts, i * block + p),
            )
            for p in range(0, block, STEP)
        ]
        return total + sum(sum_tiles(chunks))

    return lax.fori_loop(0, src.shape[0] // block, step, jnp.zeros((cols, RANK), F32))


def leaf_at(index):
    return pl.ds(pl.multiple_of(index * LEAF, LEAF), LEAF)


def order_kernel(perm, skel, events, coeffs, xs, ws, src, tgt, own, table, rows, picked):
    feat, ev_dev = events.shape
    cols = coeffs.shape[0]
    blocks = ev_dev // LEAF

    @pl.loop(0, blocks)
    def _(i):
        at = leaf_at(i)
        source = source_columns(events[:, at].astype(F32))
        table[at, :] = jnp.concatenate([source, coeffs[:, at].astype(F32)], axis=0).T

    @pl.loop(0, RANK // 8)
    def _(i):
        for u in range(8):
            j = i * 8 + u
            picked[pl.ds(j, 1), :] = table[pl.ds(perm[skel[j]], 1), :]

    own_x = picked[...].T[:feat]
    own_target = target_columns(own_x)

    def gather(i):
        for u in range(LEAF):
            j = i * LEAF + u
            rows[pl.ds(j, 1), :] = table[pl.ds(perm[j], 1), :]

    def finish(i, total):
        at = leaf_at(i)
        block = rows[at, :]
        src[at, :] = block.astype(BF16)
        block = block.T
        xs[:, at] = block[:feat].astype(BF16)
        ws[:, at] = block[SPAN:].astype(BF16)
        tgt[:, at] = target_columns(block[:feat])
        source = table[at, :].astype(BF16)
        return total + dot(coeffs[:, at], jnp.exp2(dot(source, own_target)).astype(BF16))

    def step(i, total):
        total = finish(i - 1, total)
        gather(i)
        return total

    gather(0)
    total = lax.fori_loop(1, blocks, step, jnp.zeros((cols, RANK), F32))
    total = finish(blocks - 1, total)
    own[:feat, :] = own_x.astype(BF16)
    own[feat:, :] = (total * np.float32(1.0 / ev_dev**0.5)).astype(BF16)


def exchange_kernel(
    devs,
    picks,
    xs,
    ws,
    src,
    tgt,
    own,
    skel,
    part,
    halo_src,
    left_w,
    right_w,
    left_x,
    right_x,
    low,
    terms,
    high,
    low_src,
    low_w,
    high_src,
    high_w,
    halo_send,
    halo_recv,
    low_send,
    low_recv,
    term_send,
    term_recv,
    high_send,
    high_recv,
):
    groups, nodes = devs
    feat, ev_dev = xs.shape
    cols = ws.shape[0]
    far = picks.shape[0]
    leaves = ev_dev // LEAF
    reach = REACH * LEAF
    near_scale = 16.0 / (LEAF * NEAR) ** 0.5
    low_scale = np.float32(128.0 / (far * RANK) ** 0.5 / near_scale)
    high_scale = np.float32(128.0 / (groups * RANK) ** 0.5 / near_scale)
    outer = lax.axis_index("outer")
    inner = lax.axis_index("inner")
    me = outer * nodes + inner
    after = lax.rem(me + 1, groups * nodes)
    before = lax.rem(me + groups * nodes - 1, groups * nodes)
    after = (after // nodes, lax.rem(after, nodes))
    before = (before // nodes, lax.rem(before, nodes))
    inners = [(outer, lax.rem(inner + k, nodes)) for k in range(1, nodes)]
    outers = [(lax.rem(outer + k, groups), inner) for k in range(1, groups)]
    mesh_id = pl.DeviceIdType.MESH

    barrier = pltpu.get_barrier_semaphore()
    for device in inners + outers + [after, before]:
        pl.semaphore_signal(barrier, inc=1, device_id=device, device_id_type=mesh_id)
    pl.semaphore_wait(barrier, len(inners) + len(outers) + 2)

    def send(source, target, device, send_sem, recv_sem):
        copy = pltpu.make_async_remote_copy(
            src_ref=source,
            dst_ref=target,
            send_sem=send_sem,
            recv_sem=recv_sem,
            device_id=device,
            device_id_type=mesh_id,
        )
        copy.start()
        return copy

    low_copies = [
        send(own, low.at[k + 1], device, low_send.at[k], low_recv.at[k])
        for k, device in enumerate(inners)
    ]
    low[0] = own[...]
    tail = pl.ds(ev_dev - reach, reach)
    head = pl.ds(0, reach)
    x_copies = [
        send(xs.at[:, tail], left_x, after, halo_send.at[0], halo_recv.at[0]),
        send(xs.at[:, head], right_x, before, halo_send.at[1], halo_recv.at[1]),
    ]
    def add_leaves(first, last, chunks_of, scale, fresh):
        @pl.loop(first // TURN, last // TURN)
        def _(turn):
            ats = [
                at for u in range(TURN) for at in halves_of(turn * TURN + u)
            ]
            chunks = [chunks_of(turn * TURN + i * STEP // LEAF, at) for i, at in enumerate(ats)]
            sums = sum_tiles([chunk for one in chunks for chunk in one])
            each = len(chunks[0])
            for i, at in enumerate(ats):
                total = sum(sums[i * each : (i + 1) * each])
                total = total if scale is None else total * scale
                part[:, at] = total if fresh else part[:, at] + total

    def own_chunks(leaf, at):
        return [
            (
                rows_of(src, leaf * LEAF, LEAF),
                lambda: tgt[:, at],
                columns_of(ws, leaf * LEAF, LEAF),
            )
        ]

    def low_chunks(leaf, at):
        chunks = []
        for first in range(0, far, 4):
            there = [picks[first + f, leaf] for f in range(4)]
            chunks.append(
                (
                    lambda there=there: jnp.concatenate([low_src[t] for t in there], axis=0),
                    lambda: tgt[:, at],
                    lambda there=there: jnp.concatenate([low_w[t] for t in there], axis=1),
                )
            )
        return chunks

    def high_chunks(leaf, at):
        return [(lambda: high_src[...], lambda: tgt[:, at], lambda: high_w[...])]

    half = leaves // 2
    add_leaves(0, leaves, own_chunks, None, True)

    for copy in low_copies:
        copy.wait()
    w_copies = [
        send(ws.at[:, tail], left_w, after, halo_send.at[2], halo_recv.at[2]),
        send(ws.at[:, head], right_w, before, halo_send.at[3], halo_recv.at[3]),
    ]
    for k in range(nodes):
        place = lax.rem(inner + nodes - k, nodes)
        low_src[place] = source_rows(low[k, :feat, :].astype(F32))
        low_w[place] = low[k, feat:, :]
    group_x = jnp.zeros((feat, RANK), F32)
    width = 8 * RANK
    for first in range(0, nodes, 8):
        row = lax.broadcasted_iota(jnp.int32, (width, RANK), 0) + first * RANK
        hot = jnp.where(row == skel[...], 1.0, 0.0).astype(BF16)
        points = low_src[first : first + 8].reshape(width, DEPTH)[:, :feat]
        group_x = group_x + lax.dot_general(
            points, hot, (((0,), (0,)), ((), ())), preferred_element_type=F32
        )
    total = term_of(src, ws, target_columns(group_x), cols)
    terms[0] = (total * np.float32(1.0 / (ev_dev * nodes) ** 0.5)).astype(BF16)
    term_copies = [
        send(terms.at[0], terms.at[k + 1], device, term_send.at[k], term_recv.at[k])
        for k, device in enumerate(inners)
    ]

    add_leaves(0, half, low_chunks, low_scale, False)

    for copy in term_copies:
        copy.wait()
    total = jnp.zeros((cols, RANK), F32)
    for k in range(nodes):
        total = total + terms[k].astype(F32)
    high[0, :feat, :] = group_x.astype(BF16)
    high[0, feat:, :] = total.astype(BF16)
    high_copies = [
        send(high.at[0], high.at[k + 1], device, high_send.at[k], high_recv.at[k])
        for k, device in enumerate(outers)
    ]

    add_leaves(half, leaves, low_chunks, low_scale, False)
    for copy in x_copies:
        copy.wait()

    @pl.loop(0, REACH)
    def _(i):
        for side, ref in enumerate((left_x, right_x)):
            x = ref[:, leaf_at(i)].astype(F32)
            halo_src[leaf_at(side * REACH + i), :] = source_rows(x)

    for copy in high_copies:
        copy.wait()
    for k in range(1, groups):
        at = slice((k - 1) * RANK, k * RANK)
        high_src[at, :] = source_rows(high[k, :feat, :].astype(F32))
        high_w[:, at] = high[k, feat:, :]

    add_leaves(0, leaves, high_chunks, high_scale, False)

    for copy in w_copies:
        copy.wait()


def near_kernel(
    nodes, near_list, count, tgt, ws, left_w, right_w, src_own, halo_src, part, out, src, wts,
    near, places, targets, sems,
):
    leaves = ws.shape[1] // LEAF
    cols = ws.shape[0]
    dummy = leaves + 2 * REACH
    left_at = pl.ds(0, REACH * LEAF)
    own_at = pl.ds(REACH * LEAF, leaves * LEAF)
    right_at = pl.ds((REACH + leaves) * LEAF, REACH * LEAF)
    copies = [
        pltpu.make_async_copy(source, target, sems.at[i])
        for i, (source, target) in enumerate(
            (
                (src_own, src.at[own_at, :]),
                (halo_src.at[left_at, :], src.at[left_at, :]),
                (halo_src.at[pl.ds(REACH * LEAF, REACH * LEAF), :], src.at[right_at, :]),
                (ws, wts.at[:, own_at]),
                (left_w, wts.at[:, left_at]),
                (right_w, wts.at[:, right_at]),
                (part, near),
            )
        )
    ]
    for copy in copies:
        copy.start()
    src[dummy * LEAF :, :] = jnp.zeros((LEAF, DEPTH), BF16)
    wts[:, dummy * LEAF :] = jnp.zeros((cols, LEAF), BF16)

    first = (lax.axis_index("outer") * nodes + lax.axis_index("inner")) * leaves - REACH

    def list_leaf(leaf, total):
        def list_slot(slot, at):
            places[at] = near_list[leaf, slot] - first
            targets[at] = leaf
            return at + 1

        return lax.fori_loop(1, count[leaf], list_slot, total)

    pairs = lax.fori_loop(0, leaves, list_leaf, jnp.int32(0))
    for u in range(PAIRS):
        places[pairs + u] = dummy
        targets[pairs + u] = 0
    for copy in copies:
        copy.wait()

    @pl.loop(0, lax.div(pairs + PAIRS - 1, PAIRS))
    def _(turn):
        chunks, ats = [], []
        for u in range(PAIRS):
            place = places[turn * PAIRS + u]
            for at in halves_of(targets[turn * PAIRS + u]):
                ats.append(at)
                chunks.append(
                    (
                        rows_of(src, place * LEAF, LEAF),
                        lambda at=at: tgt[:, at],
                        columns_of(wts, place * LEAF, LEAF),
                    )
                )
        for at, one in zip(ats, sum_tiles(chunks)):
            near[:, at] += one

    near_scale = np.float32(16.0 / (LEAF * NEAR) ** 0.5)

    @pl.loop(0, leaves)
    def _(leaf):
        at = leaf_at(leaf)
        out[:, at] = (near[:, at] * near_scale).astype(BF16)


def call(kernel, scalars, vectors, outs, scratch, tiles, collective_id=None, anywhere=()):
    flops = int(tiles * LEAF * LEAF * 2 * 128)
    specs = [pl.BlockSpec(memory_space=pltpu.SMEM)] * len(scalars)
    specs += [pl.BlockSpec(memory_space=pltpu.VMEM)] * len(vectors)
    specs += [pl.BlockSpec(memory_space=pl.ANY)] * len(anywhere)
    return pl.pallas_call(
        kernel,
        out_shape=outs,
        in_specs=specs,
        out_specs=jax.tree.map(lambda _: pl.BlockSpec(memory_space=pltpu.VMEM), outs),
        scratch_shapes=scratch,
        compiler_params=pltpu.CompilerParams(
            vmem_limit_bytes=VMEM_BYTES,
            collective_id=collective_id,
            has_side_effects=collective_id is not None,
        ),
        cost_estimate=pl.CostEstimate(
            flops=flops, bytes_accessed=8 << 20, transcendentals=int(tiles * LEAF * LEAF)
        ),
    )(*scalars, *vectors, *anywhere)


def per_device(events, coeffs, tree_perm, near_list, near_count, far_list, skel_low, skel_high):
    group_devs = lax.axis_size("inner")
    group_count = lax.axis_size("outer")
    feat, ev_dev = events.shape
    cols = coeffs.shape[0]
    height = feat + cols
    shape = jax.ShapeDtypeStruct

    xs, ws, src, tgt, own = call(
        order_kernel,
        (tree_perm[0], skel_low[0]),
        (events, coeffs),
        (
            shape((feat, ev_dev), BF16),
            shape((cols, ev_dev), BF16),
            shape((ev_dev, DEPTH), BF16),
            shape((DEPTH, ev_dev), BF16),
            shape((height, RANK), BF16),
        ),
        [
            pltpu.VMEM((ev_dev, 128), F32),
            pltpu.VMEM((ev_dev, 128), F32),
            pltpu.VMEM((RANK, 128), F32),
        ],
        4,
    )
    reach = REACH * LEAF
    sems = [4, 4] + [group_devs - 1] * 4 + [group_count - 1] * 2
    part, halo_src, left_w, right_w = call(
        functools.partial(exchange_kernel, (group_count, group_devs)),
        (far_list.T,),
        (xs, ws, src, tgt, own, skel_high),
        (
            shape((cols, ev_dev), F32),
            shape((2 * reach, DEPTH), BF16),
            shape((cols, reach), BF16),
            shape((cols, reach), BF16),
        ),
        [
            pltpu.VMEM((feat, reach), BF16),
            pltpu.VMEM((feat, reach), BF16),
            pltpu.VMEM((group_devs, height, RANK), BF16),
            pltpu.VMEM((group_devs, cols, RANK), BF16),
            pltpu.VMEM((group_count, height, RANK), BF16),
            pltpu.VMEM((group_devs, RANK, DEPTH), BF16),
            pltpu.VMEM((group_devs, cols, RANK), BF16),
            pltpu.VMEM(((group_count - 1) * RANK, DEPTH), BF16),
            pltpu.VMEM((cols, (group_count - 1) * RANK), BF16),
        ]
        + [pltpu.SemaphoreType.DMA((n,)) for n in sems],
        52,
        collective_id=0,
    )
    window = ev_dev + 2 * reach + LEAF
    slots = LEAF_DEV * NEAR + PAIRS
    return call(
        functools.partial(near_kernel, group_devs),
        (near_list, near_count),
        (tgt,),
        shape((cols, ev_dev), BF16),
        [
            pltpu.VMEM((window, DEPTH), BF16),
            pltpu.VMEM((cols, window), BF16),
            pltpu.VMEM((cols, ev_dev), F32),
            pltpu.SMEM((slots,), jnp.int32),
            pltpu.SMEM((slots,), jnp.int32),
            pltpu.SemaphoreType.DMA((7,)),
        ],
        100,
        anywhere=(ws, left_w, right_w, src, halo_src, part),
    )


def solution(mesh):
    return jax.shard_map(
        per_device,
        mesh=mesh,
        in_specs=(
            P(None, ("outer", "inner")),
            P(None, ("outer", "inner")),
            P(("outer", "inner"), None),
            P(("outer", "inner"), None),
            P(("outer", "inner")),
            P(("outer", "inner"), None),
            P(("outer", "inner"), None),
            P("outer", None),
        ),
        out_specs=P(None, ("outer", "inner")),
        check_vma=False,
    )
```
